32 devices in a mesh: grp: 2 (over x), row: 16 (over z, y, core).
Axes of the slice: x: 2, y: 2, z: 4, core: 2. Of those that a mesh axis runs over, the one named last changes fastest.
Arguments:
- excitations: bfloat16 [32, 8192, 128], P('grp', 'row'), parts along dimension 0, may hold values from -0.005859375 to 0.005859375
- valence_orb: bfloat16 [2048, 128], P(('grp', 'row')), parts along dimension 0, may hold values from -6 to 6
- conduction_orb: bfloat16 [2048, 8192], P(('grp', 'row')), parts along dimension 0, may hold values from -6 to 6
- screened: bfloat16 [2048, 1024], P(('grp', 'row')), parts along dimension 0, may hold values from -0.005859375 to 0.005859375
Outputs:
- action: bfloat16 [32, 8192, 128], P('grp', 'row'), parts along dimension 0
The draws below stay inside these ranges and needn't reach their ends.
There are 2 independent parts, one for each index of `grp`. The reference program is written for one: setup_inputs(seed, part) draws one part's arguments, and reference() takes and returns one part's arrays. A program takes and returns all parts, laid end to end along the dimension named above; each array names one. Nothing has to cross between parts.
All inputs are finite; a program needn't handle non-finite values.
Results may differ from the reference program's by a relative error of at most 0.0064.
Values may be sent and summed in bfloat16 or wider, within the bound.
No kernel may reach another device: no remote copies, remote signals or barrier semaphores. Data moves between devices by JAX's collectives and lax.ppermute only.
A program may use at most 64 MiB of HBM per device.

```python
import math
import jax
import jax.numpy as jnp
from jax import lax

B = 16
V = 128
C = 8192
P_SIZE = 1024


def shard_levels(own_key, shape, cuts, smallest, high):
    factor_of, own = 1.0, jax.random.fold_in(own_key, 6)
    for axis_at, blocks in cuts:
        heights = jnp.exp(jax.random.uniform(jax.random.fold_in(own, axis_at), (blocks,), jnp.float32, smallest / len(cuts), high / len(cuts)))
        factor_of = factor_of * jnp.repeat(heights, shape[axis_at] // blocks).reshape([-1 if axis == axis_at else 1 for axis in range(len(shape))])
    return factor_of


def gaussian(stream_key, extent, width, bound, pieces=(), held_as=jnp.bfloat16):
    factor_of = shard_levels(stream_key, extent, pieces, -0.22, 0.18) if pieces else 1.0
    drawn = jax.random.normal(stream_key, extent, jnp.float32) * width * factor_of
    return jnp.minimum(jnp.maximum(drawn, -bound), bound).astype(held_as)


def setup_inputs(seed: int = 0, part: int = 0) -> dict:
    arg_keys = jax.random.split(jax.random.key(seed), 5)
    part_keys = jax.random.split(jax.random.fold_in(arg_keys[4], part), 5)
    excitations = gaussian(part_keys[0], (B, C, V), (V * C) ** -0.5, 0.005859375, ((1, 16),))
    valence_orb = gaussian(part_keys[1], (P_SIZE, V), 1.0, 6.0, ((0, 16),))
    conduction_orb = gaussian(part_keys[2], (P_SIZE, C), 1.0, 6.0, ((0, 16),))
    screened = gaussian(part_keys[3], (P_SIZE, P_SIZE), (P_SIZE * P_SIZE) ** -0.5, 0.005859375, ((0, 16),))
    return {"excitations": excitations, "valence_orb": valence_orb, "conduction_orb": conduction_orb, "screened": screened}


def reference(excitations, valence_orb, conduction_orb, screened):
    span_size = math.gcd(P_SIZE, 512)
    block_count = P_SIZE // span_size
    exc = excitations.astype(jnp.float32)
    val_blocks = valence_orb.reshape(block_count, span_size, V)
    cond_blocks = conduction_orb.reshape(block_count, span_size, C)

    def density_block(blocks):
        val_block, cond_block = blocks
        mixed = jnp.einsum("bcv,mv->bmc", exc, val_block.astype(jnp.float32))
        return jnp.sum(mixed * cond_block.astype(jnp.float32)[None], axis=2)

    density = lax.map(density_block, (val_blocks, cond_blocks))
    density = density.transpose(1, 0, 2).reshape(B, P_SIZE).astype(jnp.bfloat16)
    field = jnp.dot(density, screened.T, preferred_element_type=jnp.float32).astype(jnp.bfloat16)
    field_blocks = field.reshape(B, block_count, span_size).transpose(1, 0, 2)

    def project(total, blocks):
        val_block, cond_block, field_block = blocks
        pair = (cond_block.astype(jnp.float32)[None] * field_block.astype(jnp.float32)[:, :, None]).astype(jnp.bfloat16)
        pair = lax.optimization_barrier(pair).astype(jnp.float32)
        total = total + jnp.einsum("bmc,mv->bcv", pair, val_block.astype(jnp.float32))
        return total, None

    initial = jnp.zeros((B, C, V), jnp.float32)
    total, unused = lax.scan(project, initial, (val_blocks, cond_blocks, field_blocks))
    return total.astype(jnp.bfloat16)
```

```python
import functools
import math

import jax
import jax.numpy as jnp
from jax import lax
from jax.experimental import pallas as pl
from jax.experimental.pallas import tpu as pltpu
from jax.sharding import PartitionSpec as P

AXIS = "row"
VMEM = pltpu.VMEM
NT = (((1,), (1,)), ((), ()))


def swap(x, bits, size):
    return lax.ppermute(x, AXIS, [(i, i ^ bits) for i in range(size)])


def exchange(x, step, count, size):
    return [x] + [swap(x, k * step, size) for k in range(1, count)]


def density_kernel(exc_ref, val_ref, cond_ref, out_ref):
    batch, valence, _ = exc_ref.shape
    cond, val = cond_ref[...], val_ref[...].astype(jnp.float32)
    group = math.gcd(batch, 4)
    sums = []
    for first in range(0, batch, group):
        exc = exc_ref[first : first + group].reshape(group * valence, -1)
        mixed = lax.dot_general(exc, cond, NT, preferred_element_type=jnp.float32)
        mixed = mixed.reshape(group, valence, -1) * val[None]
        sums.append(jnp.sum(mixed, axis=1))
    out_ref[...] = jnp.concatenate(sums, axis=0).astype(out_ref.dtype)


def partial_density(exc_t, val_t, cond_all):
    batch, valence, cond_local = exc_t.shape
    points = cond_all.shape[0]
    width = math.gcd(points, 1024)
    return pl.pallas_call(
        density_kernel,
        grid=(points // width,),
        in_specs=[
            pl.BlockSpec(memory_space=VMEM),
            pl.BlockSpec((valence, width), lambda i: (0, i)),
            pl.BlockSpec((width, cond_local), lambda i: (i, 0)),
        ],
        out_specs=pl.BlockSpec((batch, width), lambda i: (0, i)),
        out_shape=jax.ShapeDtypeStruct((batch, points), jnp.bfloat16),
        compiler_params=pltpu.CompilerParams(vmem_limit_bytes=24 << 20),
        cost_estimate=pl.CostEstimate(
            flops=2 * exc_t.size * points,
            bytes_accessed=2 * (exc_t.size + cond_all.size + val_t.size),
            transcendentals=0,
        ),
    )(exc_t, val_t, cond_all)


def action_kernel(z_ref, cond_ref, val_ref, *refs, layers, span):
    fields, (out_ref, held_ref, total_ref, sems) = refs[:layers], refs[layers:]
    batch = held_ref.shape[1]
    valence = val_ref.shape[0]
    for k, field in enumerate(fields):
        held_ref[z_ref[0] ^ k] = field[...].astype(jnp.float32)
    copies = []
    for first in range(0, batch, span):
        sides = []
        for b in range(first, first + span):
            row = jnp.concatenate([held_ref[k, b : b + 1, :] for k in range(layers)], axis=1)
            sides.append((val_ref[...].astype(jnp.float32) * row).astype(jnp.bfloat16))
        weights = jnp.concatenate(sides, axis=0)
        total = lax.dot_general(cond_ref[...], weights, NT, preferred_element_type=jnp.float32)
        for part in range(span):
            total_ref[first + part] = total[:, part * valence : (part + 1) * valence].astype(total_ref.dtype)
        piece = pl.ds(first, span)
        copies.append(pltpu.make_async_copy(total_ref.at[piece], out_ref.at[piece], sems.at[first // span]))
        copies[-1].start()
    for copy in copies:
        copy.wait()


def action_of(z, cond_t, val_t, fields):
    cond_local, points = cond_t.shape
    valence = val_t.shape[0]
    layers, (batch, chunk) = len(fields), fields[0].shape
    span = batch
    while span > 1 and span * valence * points * 2 > 1 << 20:
        span //= 2
    span = math.gcd(batch, span)
    whole = pl.BlockSpec(memory_space=VMEM)
    shape = (batch, cond_local, valence)
    return pl.pallas_call(
        functools.partial(action_kernel, layers=layers, span=span),
        in_specs=[pl.BlockSpec(memory_space=pltpu.SMEM)] + [whole] * (2 + layers),
        out_specs=pl.BlockSpec(memory_space=pl.ANY),
        out_shape=jax.ShapeDtypeStruct(shape, jnp.bfloat16),
        scratch_shapes=[
            pltpu.VMEM((layers, batch, chunk), jnp.float32),
            pltpu.VMEM(shape, jnp.bfloat16),
            pltpu.SemaphoreType.DMA((batch // span,)),
        ],
        compiler_params=pltpu.CompilerParams(vmem_limit_bytes=32 << 20),
        cost_estimate=pl.CostEstimate(
            flops=2 * batch * valence * cond_local * points,
            bytes_accessed=2 * (cond_t.size + val_t.size + batch * cond_local * valence),
            transcendentals=0,
        ),
    )(z, cond_t, val_t, *fields)


def body(size, excitations, valence_orb, conduction_orb, screened):
    batch, cond_local, valence = excitations.shape
    rows = valence_orb.shape[0]
    points = rows * size
    q_size = 1 << ((size.bit_length() - 1) // 2)
    z_size = size // q_size
    index = lax.axis_index(AXIS)
    z, q = index // q_size, index % q_size

    blocks = conduction_orb.reshape(rows, size, cond_local).transpose(1, 0, 2)
    blocks, valence_orb, screened = lax.optimization_barrier((blocks, valence_orb, screened))
    cond_all = lax.all_to_all(blocks, AXIS, split_axis=0, concat_axis=0, tiled=True)
    cond_all = cond_all.reshape(points, cond_local)

    val = jnp.concatenate(exchange(valence_orb, q_size, z_size, size), axis=0)
    val = jnp.stack(exchange(val, 1, q_size, size)).reshape(size, rows, valence)
    val = jnp.concatenate(
        [val[((i % q_size) ^ q) * z_size + ((i // q_size) ^ z)] for i in range(size)], axis=0
    )
    val_t = val.T
    scr = jnp.stack(exchange(screened, 1, q_size, size))
    scr = jnp.concatenate([scr[k ^ q] for k in range(q_size)], axis=0)
    exc_t = excitations.transpose(0, 2, 1)

    density = partial_density(exc_t, val_t, cond_all)
    density = sum(d.astype(jnp.float32) for d in exchange(density, q_size, z_size, size))
    partial = lax.dot_general(
        density.astype(jnp.bfloat16), scr, NT, preferred_element_type=jnp.float32
    )
    sent = partial.astype(jnp.bfloat16)
    field = partial + sum(f.astype(jnp.float32) for f in exchange(sent, 1, q_size, size)[1:])
    fields = exchange(field.astype(jnp.bfloat16), q_size, z_size, size)
    return action_of(z.reshape(1), cond_all.T, val_t, fields)


def solution(mesh):
    in_specs = (
        P("grp", "row", None),
        P(("grp", "row"), None),
        P(("grp", "row"), None),
        P(("grp", "row"), None),
    )
    out_specs = P("grp", "row", None)
    size = mesh.shape[AXIS]
    return jax.shard_map(
        functools.partial(body, size),
        mesh=mesh,
        in_specs=in_specs,
        out_specs=out_specs,
        check_vma=False,
    )
```

```python
import functools
import math

import jax
import jax.numpy as jnp
from jax import lax
from jax.experimental import pallas as pl
from jax.experimental.pallas import tpu as pltpu
from jax.sharding import PartitionSpec as P

AXIS = "row"
VMEM = pltpu.VMEM
NT = (((1,), (1,)), ((), ()))


def swap(x, bits, size):
    return lax.ppermute(x, AXIS, [(i, i ^ bits) for i in range(size)])


def exchange(x, step, count, size):
    return [x] + [swap(x, k * step, size) for k in range(1, count)]


def density_kernel(exc_ref, val_ref, cond_ref, out_ref):
    batch, valence, _ = exc_ref.shape
    cond, val = cond_ref[...], val_ref[...].astype(jnp.float32)
    group = math.gcd(batch, 4)
    sums = []
    for first in range(0, batch, group):
        exc = exc_ref[first : first + group].reshape(group * valence, -1)
        mixed = lax.dot_general(exc, cond, NT, preferred_element_type=jnp.float32)
        mixed = mixed.reshape(group, valence, -1) * val[None]
        sums.append(jnp.sum(mixed, axis=1))
    out_ref[...] = jnp.concatenate(sums, axis=0).astype(out_ref.dtype)


def partial_density(exc_t, val_t, cond_all):
    batch, valence, cond_local = exc_t.shape
    points = cond_all.shape[0]
    width = math.gcd(points, 1024)
    return pl.pallas_call(
        density_kernel,
        grid=(points // width,),
        in_specs=[
            pl.BlockSpec(memory_space=VMEM),
            pl.BlockSpec((valence, width), lambda i: (0, i)),
            pl.BlockSpec((width, cond_local), lambda i: (i, 0)),
        ],
        out_specs=pl.BlockSpec((batch, width), lambda i: (0, i)),
        out_shape=jax.ShapeDtypeStruct((batch, points), jnp.bfloat16),
        compiler_params=pltpu.CompilerParams(vmem_limit_bytes=16 << 20),
        cost_estimate=pl.CostEstimate(
            flops=2 * exc_t.size * points,
            bytes_accessed=2 * (exc_t.size + cond_all.size + val_t.size),
            transcendentals=0,
        ),
    )(exc_t, val_t, cond_all)


def action_kernel(z_ref, cond_ref, val_ref, *refs, layers, span):
    fields, (out_ref, held_ref, total_ref, sems) = refs[:layers], refs[layers:]
    batch = held_ref.shape[1]
    valence = val_ref.shape[0]
    for k, field in enumerate(fields):
        held_ref[z_ref[0] ^ k] = field[...].astype(jnp.float32)
    copies = []
    for first in range(0, batch, span):
        sides = []
        for b in range(first, first + span):
            row = jnp.concatenate([held_ref[k, b : b + 1, :] for k in range(layers)], axis=1)
            sides.append((val_ref[...].astype(jnp.float32) * row).astype(jnp.bfloat16))
        weights = jnp.concatenate(sides, axis=0)
        total = lax.dot_general(cond_ref[...], weights, NT, preferred_element_type=jnp.float32)
        for part in range(span):
            total_ref[first + part] = total[:, part * valence : (part + 1) * valence].astype(total_ref.dtype)
        piece = pl.ds(first, span)
        copies.append(pltpu.make_async_copy(total_ref.at[piece], out_ref.at[piece], sems.at[first // span]))
        copies[-1].start()
    for copy in copies:
        copy.wait()


def action_of(z, cond_t, val_t, fields):
    cond_local, points = cond_t.shape
    valence = val_t.shape[0]
    layers, (batch, chunk) = len(fields), fields[0].shape
    span = batch
    while span > 1 and span * valence * points * 2 > 1 << 20:
        span //= 2
    span = math.gcd(batch, span)
    whole = pl.BlockSpec(memory_space=VMEM)
    shape = (batch, cond_local, valence)
    return pl.pallas_call(
        functools.partial(action_kernel, layers=layers, span=span),
        in_specs=[pl.BlockSpec(memory_space=pltpu.SMEM)] + [whole] * (2 + layers),
        out_specs=pl.BlockSpec(memory_space=pl.ANY),
        out_shape=jax.ShapeDtypeStruct(shape, jnp.bfloat16),
        scratch_shapes=[
            pltpu.VMEM((layers, batch, chunk), jnp.float32),
            pltpu.VMEM(shape, jnp.bfloat16),
            pltpu.SemaphoreType.DMA((batch // span,)),
        ],
        compiler_params=pltpu.CompilerParams(vmem_limit_bytes=16 << 20),
        cost_estimate=pl.CostEstimate(
            flops=2 * batch * valence * cond_local * points,
            bytes_accessed=2 * (cond_t.size + val_t.size + batch * cond_local * valence),
            transcendentals=0,
        ),
    )(z, cond_t, val_t, *fields)


def body_whole(size, excitations, valence_orb, conduction_orb, screened):
    batch, cond_local, valence = excitations.shape
    rows = valence_orb.shape[0]
    points = rows * size
    q_size = 1 << ((size.bit_length() - 1) // 2)
    z_size = size // q_size
    index = lax.axis_index(AXIS)
    z, q = index // q_size, index % q_size

    blocks = conduction_orb.reshape(rows, size, cond_local).transpose(1, 0, 2)
    blocks, valence_orb, screened = lax.optimization_barrier((blocks, valence_orb, screened))
    cond_all = lax.all_to_all(blocks, AXIS, split_axis=0, concat_axis=0, tiled=True)
    cond_all = cond_all.reshape(points, cond_local)

    val = jnp.concatenate(exchange(valence_orb, q_size, z_size, size), axis=0)
    val = jnp.stack(exchange(val, 1, q_size, size)).reshape(size, rows, valence)
    val = jnp.concatenate(
        [val[((i % q_size) ^ q) * z_size + ((i // q_size) ^ z)] for i in range(size)], axis=0
    )
    val_t = val.T
    scr = jnp.stack(exchange(screened, 1, q_size, size))
    scr = jnp.concatenate([scr[k ^ q] for k in range(q_size)], axis=0)
    exc_t = excitations.transpose(0, 2, 1)

    density = partial_density(exc_t, val_t, cond_all)
    density = sum(d.astype(jnp.float32) for d in exchange(density, q_size, z_size, size))
    partial = lax.dot_general(
        density.astype(jnp.bfloat16), scr, NT, preferred_element_type=jnp.float32
    )
    sent = partial.astype(jnp.bfloat16)
    field = partial + sum(f.astype(jnp.float32) for f in exchange(sent, 1, q_size, size)[1:])
    fields = exchange(field.astype(jnp.bfloat16), q_size, z_size, size)
    return action_of(z.reshape(1), cond_all.T, val_t, fields)


def slabs_of(index, cond, val, screened, chips, near):
    width = cond.shape[1] // (2 * chips)
    slabs = []
    for k in range(chips):
        parts = [lax.dynamic_slice_in_dim(cond, (index ^ j) * width, width, 1) for j in (2 * k, 2 * k + 1)]
        slabs.append(jnp.concatenate(parts + [val] + [screened] * (k < near), axis=1))
    return slabs


def pack_kernel(*refs, first, middle):
    *slabs, out_ref = refs
    at = 0
    for start, stop in [(first, middle), (middle, None)]:
        for slab in slabs:
            columns = (stop or slab.shape[1]) - start
            if columns:
                out_ref[:, at : at + columns] = slab[:, start : start + columns]
                at += columns


def pack(slabs, first, middle):
    columns = sum(slab.shape[1] for slab in slabs) - first * len(slabs)
    whole = pl.BlockSpec(memory_space=VMEM)
    return pl.pallas_call(
        functools.partial(pack_kernel, first=first, middle=middle),
        in_specs=[whole] * len(slabs),
        out_specs=whole,
        out_shape=jax.ShapeDtypeStruct((slabs[0].shape[0], columns), slabs[0].dtype),
        compiler_params=pltpu.CompilerParams(vmem_limit_bytes=8 << 20),
        cost_estimate=pl.CostEstimate(flops=0, bytes_accessed=1 << 20, transcendentals=0),
    )(*slabs)


def density_part_kernel(*refs, blocks, val_at, step):
    exc_ref, sources, (out_ref, cond_ref, val_ref) = refs[0], refs[1:-3], refs[-3:]
    batch, valence, width = exc_ref.shape
    rows = sources[0].shape[0]
    val = []
    for k in range(blocks):
        source, start = (sources[k], 0) if len(sources) > 1 else (sources[0], k * step)
        cond_ref[k * rows : (k + 1) * rows, :] = source[:, start : start + width]
        val.append(source[:, start + val_at : start + val_at + valence])
    val = jnp.concatenate(val, axis=0).T
    val_ref[...] = val
    val = val.astype(jnp.float32)
    part = math.gcd(batch, 4)
    sums = []
    for first in range(0, batch, part):
        exc = exc_ref[first : first + part].reshape(part * valence, width)
        mixed = lax.dot_general(exc, cond_ref[...], NT, preferred_element_type=jnp.float32)
        mixed = mixed.reshape(part, valence, -1) * val[None]
        sums.append(jnp.sum(mixed, axis=1))
    out_ref[...] = jnp.concatenate(sums, axis=0).astype(out_ref.dtype)


def density_part(exc_t, sources, blocks, val_at, step):
    batch, valence, width = exc_t.shape
    points = blocks * sources[0].shape[0]
    whole = pl.BlockSpec(memory_space=VMEM)
    shapes = [(batch, points), (points, width), (valence, points)]
    return pl.pallas_call(
        functools.partial(density_part_kernel, blocks=blocks, val_at=val_at, step=step),
        in_specs=[whole] * (1 + len(sources)),
        out_specs=[whole] * len(shapes),
        out_shape=[jax.ShapeDtypeStruct(shape, jnp.bfloat16) for shape in shapes],
        compiler_params=pltpu.CompilerParams(vmem_limit_bytes=16 << 20),
        cost_estimate=pl.CostEstimate(
            flops=2 * exc_t.size * points, bytes_accessed=2 * exc_t.size, transcendentals=0
        ),
    )(exc_t, *sources)


def turned(x, flag):
    return jnp.where(flag, jnp.concatenate([x[:, x.shape[1] // 2 :], x[:, : x.shape[1] // 2]], axis=1), x)


def field_kernel(index_ref, *refs, z_size, near, start, rows):
    densities, screened, (forwarded, out_ref, held_ref) = refs[:z_size], refs[z_size:-3], refs[-3:]
    points = held_ref.shape[1]
    pair, chips = 2 * rows, points // (2 * rows)
    chip, core = index_ref[0] // 2, index_ref[0] % 2
    for k in range(chips):
        total = None
        for layer in range(z_size):
            at = (k ^ (layer * near)) * rows
            ref = densities[layer]
            halves = [ref[:, at + c * points // 2 : at + c * points // 2 + rows] for c in range(2)]
            term = jnp.concatenate(halves, axis=1).astype(jnp.float32)
            total = term if total is None else total + term
        place = pl.ds(pl.multiple_of((chip ^ k) * pair, pair), pair)
        held_ref[:, place] = turned(total, core == 1)
    density = held_ref[...].astype(jnp.bfloat16)
    for k in range(near):
        slab = screened[k]
        at = start + k * points
        both = [slab[:, slab.shape[1] - points :], forwarded[:, at : at + points]]
        both = jnp.concatenate(both, axis=0)
        partial = lax.dot_general(density, both, NT, preferred_element_type=jnp.float32)
        place = pl.ds(pl.multiple_of(((chip % near) ^ k) * pair, pair), pair)
        partial = turned(partial, core == 1).astype(out_ref.dtype)
        for target in range(out_ref.shape[0]):
            out_ref[target, :, place] = partial


def field_of(index, densities, screened, forwarded, copies, start):
    batch, points = densities[0].shape
    near, rows = len(screened), screened[0].shape[0]
    whole = pl.BlockSpec(memory_space=VMEM)
    columns = 2 * near * rows
    return pl.pallas_call(
        functools.partial(field_kernel, z_size=len(densities), near=near, start=start, rows=rows),
        in_specs=[pl.BlockSpec(memory_space=pltpu.SMEM)] + [whole] * (len(densities) + near + 1),
        out_specs=whole,
        out_shape=jax.ShapeDtypeStruct((copies, batch, columns), jnp.bfloat16),
        scratch_shapes=[pltpu.VMEM((batch, points), jnp.float32)],
        compiler_params=pltpu.CompilerParams(vmem_limit_bytes=16 << 20),
        cost_estimate=pl.CostEstimate(
            flops=2 * batch * points * columns, bytes_accessed=2 * points * columns, transcendentals=0
        ),
    )(index, *densities, *screened, forwarded)


def project_kernel(index_ref, field_ref, *refs, parts, span):
    conds, vals = refs[:parts], refs[parts : 2 * parts]
    out_ref, pairs_ref, total_ref, sems = refs[2 * parts :]
    size, batch, chunk = field_ref.shape
    chips, _, pair = pairs_ref.shape
    near = chunk // pair
    q_size = 2 * near
    valence = vals[0].shape[0]
    chip, core = index_ref[0] // 2, index_ref[0] % 2
    for layer in range(size // q_size):
        field = sum(field_ref[layer * q_size + k].astype(jnp.float32) for k in range(q_size))
        for k in range(near):
            pairs_ref[layer * near + k] = field[:, k * pair : (k + 1) * pair]
    both = [turned(pairs_ref[chip ^ k], core == 1) for k in range(chips)]
    halves = [x[:, : pair // 2] for x in both] + [x[:, pair // 2 :] for x in both]
    field = jnp.concatenate(halves, axis=1)
    field = field.astype(jnp.bfloat16).astype(jnp.float32)
    copies = []
    for first in range(0, batch, span):
        total, at = None, 0
        for cond, val in zip(conds, vals):
            stop = at + val.shape[1]
            sides = [
                (val[...].astype(jnp.float32) * field[b : b + 1, at:stop]).astype(jnp.bfloat16)
                for b in range(first, first + span)
            ]
            weights = jnp.concatenate(sides, axis=0)
            term = jnp.dot(weights, cond[...], preferred_element_type=jnp.float32)
            total, at = term if total is None else total + term, stop
        total = total.astype(total_ref.dtype)
        for part in range(span):
            total_ref[first + part] = total[part * valence : (part + 1) * valence].T
        piece = pl.ds(first, span)
        copies.append(pltpu.make_async_copy(total_ref.at[piece], out_ref.at[piece], sems.at[first // span]))
        copies[-1].start()
    for copy in copies:
        copy.wait()


def project(index, field, conds, vals):
    size, batch, _ = field.shape
    points, width = sum(cond.shape[0] for cond in conds), conds[0].shape[1]
    valence, span = vals[0].shape[0], math.gcd(batch, 4)
    whole = pl.BlockSpec(memory_space=VMEM)
    shape = (batch, width, valence)
    return pl.pallas_call(
        functools.partial(project_kernel, parts=len(conds), span=span),
        in_specs=[pl.BlockSpec(memory_space=pltpu.SMEM)] + [whole] * (1 + 2 * len(conds)),
        out_specs=pl.BlockSpec(memory_space=pl.ANY),
        out_shape=jax.ShapeDtypeStruct(shape, jnp.bfloat16),
        scratch_shapes=[
            pltpu.VMEM((size // 2, batch, 2 * points // size), jnp.float32),
            pltpu.VMEM(shape, jnp.bfloat16),
            pltpu.SemaphoreType.DMA((batch // span,)),
        ],
        compiler_params=pltpu.CompilerParams(vmem_limit_bytes=16 << 20),
        cost_estimate=pl.CostEstimate(
            flops=2 * batch * valence * width * points,
            bytes_accessed=2 * batch * width * valence,
            transcendentals=0,
        ),
    )(index, field, *conds, *vals)


def body_slabs(size, excitations, valence_orb, conduction_orb, screened):
    batch, width, valence = excitations.shape
    q_size = 1 << ((size.bit_length() - 1) // 2)
    z_size = size // q_size
    chips = size // 2
    index = lax.axis_index(AXIS)
    place = index.reshape(1)

    half, near = chips // 2, q_size // 2
    slabs = slabs_of(index, conduction_orb, valence_orb, screened, chips, near)
    slabs = [slabs[0]] + [swap(slabs[k], 2 * k, size) for k in range(1, chips)]
    exc_t = excitations.transpose(0, 2, 1)

    exc_t, *slabs = lax.optimization_barrier((exc_t, *slabs))
    lead = width + valence
    other = swap(pack(slabs, width, 2 * width + valence), 1, size)
    straight, cond, val = density_part(exc_t, slabs, chips, 2 * width, 0)
    turned_in, cond_other, val_other = density_part(exc_t, [other], chips, width, lead)
    density = jnp.concatenate([straight, turned_in], axis=1)

    densities = exchange(density, q_size, z_size, size)
    field = field_of(place, densities, slabs[:near], other, size, chips * lead)
    field = lax.all_to_all(field, AXIS, split_axis=0, concat_axis=0, tiled=True)
    return project(place, field, [cond, cond_other], [val, val_other])


def body(size, excitations, valence_orb, conduction_orb, screened):
    powers = size >= 8 and size & (size - 1) == 0
    aligned = excitations.shape[1] % 128 == 0 and (2 * valence_orb.shape[0]) % 128 == 0
    run = body_slabs if powers and aligned else body_whole
    return run(size, excitations, valence_orb, conduction_orb, screened)


def solution(mesh):
    in_specs = (
        P("grp", "row", None),
        P(("grp", "row"), None),
        P(("grp", "row"), None),
        P(("grp", "row"), None),
    )
    out_specs = P("grp", "row", None)
    size = mesh.shape[AXIS]
    return jax.shard_map(
        functools.partial(body, size),
        mesh=mesh,
        in_specs=in_specs,
        out_specs=out_specs,
        check_vma=False,
    )
```

```python
import functools
import math

import jax
import jax.numpy as jnp
from jax import lax
from jax.experimental import pallas as pl
from jax.experimental.pallas import tpu as pltpu
from jax.sharding import PartitionSpec as P

AXIS = "row"
VMEM = pltpu.VMEM
NT = (((1,), (1,)), ((), ()))


def swap(x, bits, size):
    return lax.ppermute(x, AXIS, [(i, i ^ bits) for i in range(size)])


def exchange(x, step, count, size):
    return [x] + [swap(x, k * step, size) for k in range(1, count)]


def density_kernel(exc_ref, val_ref, cond_ref, out_ref):
    batch, valence, _ = exc_ref.shape
    cond, val = cond_ref[...], val_ref[...].astype(jnp.float32)
    group = math.gcd(batch, 4)
    sums = []
    for first in range(0, batch, group):
        exc = exc_ref[first : first + group].reshape(group * valence, -1)
        mixed = lax.dot_general(exc, cond, NT, preferred_element_type=jnp.float32)
        mixed = mixed.reshape(group, valence, -1) * val[None]
        sums.append(jnp.sum(mixed, axis=1))
    out_ref[...] = jnp.concatenate(sums, axis=0).astype(out_ref.dtype)


def partial_density(exc_t, val_t, cond_all):
    batch, valence, cond_local = exc_t.shape
    points = cond_all.shape[0]
    width = math.gcd(points, 1024)
    return pl.pallas_call(
        density_kernel,
        grid=(points // width,),
        in_specs=[
            pl.BlockSpec(memory_space=VMEM),
            pl.BlockSpec((valence, width), lambda i: (0, i)),
            pl.BlockSpec((width, cond_local), lambda i: (i, 0)),
        ],
        out_specs=pl.BlockSpec((batch, width), lambda i: (0, i)),
        out_shape=jax.ShapeDtypeStruct((batch, points), jnp.bfloat16),
        compiler_params=pltpu.CompilerParams(vmem_limit_bytes=16 << 20),
        cost_estimate=pl.CostEstimate(
            flops=2 * exc_t.size * points,
            bytes_accessed=2 * (exc_t.size + cond_all.size + val_t.size),
            transcendentals=0,
        ),
    )(exc_t, val_t, cond_all)


def action_kernel(z_ref, cond_ref, val_ref, *refs, layers, span):
    fields, (out_ref, held_ref, total_ref, sems) = refs[:layers], refs[layers:]
    batch = held_ref.shape[1]
    valence = val_ref.shape[0]
    for k, field in enumerate(fields):
        held_ref[z_ref[0] ^ k] = field[...].astype(jnp.float32)
    copies = []
    for first in range(0, batch, span):
        sides = []
        for b in range(first, first + span):
            row = jnp.concatenate([held_ref[k, b : b + 1, :] for k in range(layers)], axis=1)
            sides.append((val_ref[...].astype(jnp.float32) * row).astype(jnp.bfloat16))
        weights = jnp.concatenate(sides, axis=0)
        total = lax.dot_general(cond_ref[...], weights, NT, preferred_element_type=jnp.float32)
        for part in range(span):
            total_ref[first + part] = total[:, part * valence : (part + 1) * valence].astype(total_ref.dtype)
        piece = pl.ds(first, span)
        copies.append(pltpu.make_async_copy(total_ref.at[piece], out_ref.at[piece], sems.at[first // span]))
        copies[-1].start()
    for copy in copies:
        copy.wait()


def action_of(z, cond_t, val_t, fields):
    cond_local, points = cond_t.shape
    valence = val_t.shape[0]
    layers, (batch, chunk) = len(fields), fields[0].shape
    span = batch
    while span > 1 and span * valence * points * 2 > 1 << 20:
        span //= 2
    span = math.gcd(batch, span)
    whole = pl.BlockSpec(memory_space=VMEM)
    shape = (batch, cond_local, valence)
    return pl.pallas_call(
        functools.partial(action_kernel, layers=layers, span=span),
        in_specs=[pl.BlockSpec(memory_space=pltpu.SMEM)] + [whole] * (2 + layers),
        out_specs=pl.BlockSpec(memory_space=pl.ANY),
        out_shape=jax.ShapeDtypeStruct(shape, jnp.bfloat16),
        scratch_shapes=[
            pltpu.VMEM((layers, batch, chunk), jnp.float32),
            pltpu.VMEM(shape, jnp.bfloat16),
            pltpu.SemaphoreType.DMA((batch // span,)),
        ],
        compiler_params=pltpu.CompilerParams(vmem_limit_bytes=16 << 20),
        cost_estimate=pl.CostEstimate(
            flops=2 * batch * valence * cond_local * points,
            bytes_accessed=2 * (cond_t.size + val_t.size + batch * cond_local * valence),
            transcendentals=0,
        ),
    )(z, cond_t, val_t, *fields)


def body_whole(size, excitations, valence_orb, conduction_orb, screened):
    batch, cond_local, valence = excitations.shape
    rows = valence_orb.shape[0]
    points = rows * size
    q_size = 1 << ((size.bit_length() - 1) // 2)
    z_size = size // q_size
    index = lax.axis_index(AXIS)
    z, q = index // q_size, index % q_size

    blocks = conduction_orb.reshape(rows, size, cond_local).transpose(1, 0, 2)
    blocks, valence_orb, screened = lax.optimization_barrier((blocks, valence_orb, screened))
    cond_all = lax.all_to_all(blocks, AXIS, split_axis=0, concat_axis=0, tiled=True)
    cond_all = cond_all.reshape(points, cond_local)

    val = jnp.concatenate(exchange(valence_orb, q_size, z_size, size), axis=0)
    val = jnp.stack(exchange(val, 1, q_size, size)).reshape(size, rows, valence)
    val = jnp.concatenate(
        [val[((i % q_size) ^ q) * z_size + ((i // q_size) ^ z)] for i in range(size)], axis=0
    )
    val_t = val.T
    scr = jnp.stack(exchange(screened, 1, q_size, size))
    scr = jnp.concatenate([scr[k ^ q] for k in range(q_size)], axis=0)
    exc_t = excitations.transpose(0, 2, 1)

    density = partial_density(exc_t, val_t, cond_all)
    density = sum(d.astype(jnp.float32) for d in exchange(density, q_size, z_size, size))
    partial = lax.dot_general(
        density.astype(jnp.bfloat16), scr, NT, preferred_element_type=jnp.float32
    )
    sent = partial.astype(jnp.bfloat16)
    field = partial + sum(f.astype(jnp.float32) for f in exchange(sent, 1, q_size, size)[1:])
    fields = exchange(field.astype(jnp.bfloat16), q_size, z_size, size)
    return action_of(z.reshape(1), cond_all.T, val_t, fields)


def pack_kernel(index_ref, *refs, width, half):
    *slabs, out_ref = refs
    other = pl.ds(pl.multiple_of((1 - index_ref[0] % 2) * width, 128), width)
    at = 0
    for slab in slabs:
        out_ref[:, at : at + width] = slab[:, other]
        at += width
    valence = min(slab.shape[1] for slab in slabs[:half]) - 2 * width
    for first, extra in ((2 * width, valence), (2 * width + valence, None)):
        for slab in slabs[:half]:
            columns = extra or slab.shape[1] - first
            if columns:
                out_ref[:, at : at + columns] = slab[:, first : first + columns]
                at += columns


def pack(index, slabs, width):
    half = len(slabs) // 2
    columns = sum(slab.shape[1] for slab in slabs) - width * len(slabs)
    whole = pl.BlockSpec(memory_space=VMEM)
    return pl.pallas_call(
        functools.partial(pack_kernel, width=width, half=half),
        in_specs=[pl.BlockSpec(memory_space=pltpu.SMEM)] + [whole] * len(slabs),
        out_specs=whole,
        out_shape=jax.ShapeDtypeStruct((slabs[0].shape[0], columns), slabs[0].dtype),
        compiler_params=pltpu.CompilerParams(vmem_limit_bytes=8 << 20),
        cost_estimate=pl.CostEstimate(flops=0, bytes_accessed=1 << 20, transcendentals=0),
    )(index, *slabs)


def density_part_kernel(index_ref, *refs, blocks):
    exc_ref, sources, (out_ref, cond_ref, val_ref) = refs[0], refs[1:-3], refs[-3:]
    batch, valence, width = exc_ref.shape
    rows = sources[0].shape[0]
    val = []
    mine = pl.ds(pl.multiple_of(index_ref[0] % 2 * width, 128), width)
    half = blocks // 2
    for k in range(blocks):
        far, near = k // half, k % half
        if len(sources) > 1:
            cond, val_source, start = sources[k][:, mine], sources[near], 2 * width + far * valence
        else:
            cond, val_source = sources[0][:, k * width : (k + 1) * width], sources[0]
            start = blocks * width + (2 * near + far) * valence
        cond_ref[k * rows : (k + 1) * rows, :] = cond
        val.append(val_source[:, start : start + valence])
    val = jnp.concatenate(val, axis=0).T
    val_ref[...] = val
    val = val.astype(jnp.float32)
    part = math.gcd(batch, 4)
    sums = []
    for first in range(0, batch, part):
        exc = exc_ref[first : first + part].reshape(part * valence, width)
        mixed = lax.dot_general(exc, cond_ref[...], NT, preferred_element_type=jnp.float32)
        mixed = mixed.reshape(part, valence, -1) * val[None]
        sums.append(jnp.sum(mixed, axis=1))
    out_ref[...] = jnp.concatenate(sums, axis=0).astype(out_ref.dtype)


def density_part(index, exc_t, sources, blocks):
    batch, valence, width = exc_t.shape
    points = blocks * sources[0].shape[0]
    whole = pl.BlockSpec(memory_space=VMEM)
    shapes = [(batch, points), (points, width), (valence, points)]
    return pl.pallas_call(
        functools.partial(density_part_kernel, blocks=blocks),
        in_specs=[pl.BlockSpec(memory_space=pltpu.SMEM)] + [whole] * (1 + len(sources)),
        out_specs=[whole] * len(shapes),
        out_shape=[jax.ShapeDtypeStruct(shape, jnp.bfloat16) for shape in shapes],
        compiler_params=pltpu.CompilerParams(vmem_limit_bytes=16 << 20),
        cost_estimate=pl.CostEstimate(
            flops=2 * exc_t.size * points, bytes_accessed=2 * exc_t.size, transcendentals=0
        ),
    )(index, exc_t, *sources)


def turned(x, flag):
    return jnp.where(flag, jnp.concatenate([x[:, x.shape[1] // 2 :], x[:, : x.shape[1] // 2]], axis=1), x)


def field_kernel(index_ref, *refs, z_size, near, start, rows):
    densities, screened, (forwarded, out_ref, held_ref) = refs[:z_size], refs[z_size:-3], refs[-3:]
    points = held_ref.shape[1]
    pair, chips = 2 * rows, points // (2 * rows)
    chip, core = index_ref[0] // 2, index_ref[0] % 2
    for k in range(chips):
        total = None
        for layer in range(z_size):
            at = (k ^ (layer * near)) * rows
            ref = densities[layer]
            halves = [ref[:, at + c * points // 2 : at + c * points // 2 + rows] for c in range(2)]
            term = jnp.concatenate(halves, axis=1).astype(jnp.float32)
            total = term if total is None else total + term
        place = pl.ds(pl.multiple_of((chip ^ k) * pair, pair), pair)
        held_ref[:, place] = turned(total, core == 1)
    density = held_ref[...].astype(jnp.bfloat16)
    for k in range(near):
        slab = screened[k]
        at = start + k * points
        both = [slab[:, slab.shape[1] - points :], forwarded[:, at : at + points]]
        both = jnp.concatenate(both, axis=0)
        partial = lax.dot_general(density, both, NT, preferred_element_type=jnp.float32)
        place = pl.ds(pl.multiple_of(((chip % near) ^ k) * pair, pair), pair)
        partial = turned(partial, core == 1).astype(out_ref.dtype)
        for target in range(out_ref.shape[0]):
            out_ref[target, :, place] = partial


def field_of(index, densities, screened, forwarded, copies, start):
    batch, points = densities[0].shape
    near, rows = len(screened), screened[0].shape[0]
    whole = pl.BlockSpec(memory_space=VMEM)
    columns = 2 * near * rows
    return pl.pallas_call(
        functools.partial(field_kernel, z_size=len(densities), near=near, start=start, rows=rows),
        in_specs=[pl.BlockSpec(memory_space=pltpu.SMEM)] + [whole] * (len(densities) + near + 1),
        out_specs=whole,
        out_shape=jax.ShapeDtypeStruct((copies, batch, columns), jnp.bfloat16),
        scratch_shapes=[pltpu.VMEM((batch, points), jnp.float32)],
        compiler_params=pltpu.CompilerParams(vmem_limit_bytes=16 << 20),
        cost_estimate=pl.CostEstimate(
            flops=2 * batch * points * columns, bytes_accessed=2 * points * columns, transcendentals=0
        ),
    )(index, *densities, *screened, forwarded)


def project_kernel(index_ref, field_ref, *refs, parts, span):
    conds, vals = refs[:parts], refs[parts : 2 * parts]
    out_ref, pairs_ref, total_ref, sems = refs[2 * parts :]
    size, batch, chunk = field_ref.shape
    chips, _, pair = pairs_ref.shape
    near = chunk // pair
    q_size = 2 * near
    valence = vals[0].shape[0]
    chip, core = index_ref[0] // 2, index_ref[0] % 2
    for layer in range(size // q_size):
        field = sum(field_ref[layer * q_size + k].astype(jnp.float32) for k in range(q_size))
        for k in range(near):
            pairs_ref[layer * near + k] = field[:, k * pair : (k + 1) * pair]
    both = [turned(pairs_ref[chip ^ k], core == 1) for k in range(chips)]
    halves = [x[:, : pair // 2] for x in both] + [x[:, pair // 2 :] for x in both]
    field = jnp.concatenate(halves, axis=1)
    field = field.astype(jnp.bfloat16).astype(jnp.float32)
    copies = []
    for first in range(0, batch, span):
        total, at = None, 0
        for cond, val in zip(conds, vals):
            stop = at + val.shape[1]
            sides = [
                (val[...].astype(jnp.float32) * field[b : b + 1, at:stop]).astype(jnp.bfloat16)
                for b in range(first, first + span)
            ]
            weights = jnp.concatenate(sides, axis=0)
            term = jnp.dot(weights, cond[...], preferred_element_type=jnp.float32)
            total, at = term if total is None else total + term, stop
        total = total.astype(total_ref.dtype)
        for part in range(span):
            total_ref[first + part] = total[part * valence : (part + 1) * valence].T
        piece = pl.ds(first, span)
        copies.append(pltpu.make_async_copy(total_ref.at[piece], out_ref.at[piece], sems.at[first // span]))
        copies[-1].start()
    for copy in copies:
        copy.wait()


def project(index, field, conds, vals):
    size, batch, _ = field.shape
    points, width = sum(cond.shape[0] for cond in conds), conds[0].shape[1]
    valence, span = vals[0].shape[0], math.gcd(batch, 4)
    whole = pl.BlockSpec(memory_space=VMEM)
    shape = (batch, width, valence)
    return pl.pallas_call(
        functools.partial(project_kernel, parts=len(conds), span=span),
        in_specs=[pl.BlockSpec(memory_space=pltpu.SMEM)] + [whole] * (1 + 2 * len(conds)),
        out_specs=pl.BlockSpec(memory_space=pl.ANY),
        out_shape=jax.ShapeDtypeStruct(shape, jnp.bfloat16),
        scratch_shapes=[
            pltpu.VMEM((size // 2, batch, 2 * points // size), jnp.float32),
            pltpu.VMEM(shape, jnp.bfloat16),
            pltpu.SemaphoreType.DMA((batch // span,)),
        ],
        compiler_params=pltpu.CompilerParams(vmem_limit_bytes=16 << 20),
        cost_estimate=pl.CostEstimate(
            flops=2 * batch * valence * width * points,
            bytes_accessed=2 * batch * width * valence,
            transcendentals=0,
        ),
    )(index, field, *conds, *vals)


def body_slabs(size, excitations, valence_orb, conduction_orb, screened):
    batch, width, valence = excitations.shape
    q_size = 1 << ((size.bit_length() - 1) // 2)
    z_size = size // q_size
    chips = size // 2
    index = lax.axis_index(AXIS)
    place = index.reshape(1)

    half, near = chips // 2, q_size // 2
    exc_t = excitations.transpose(0, 2, 1)

    def columns(x, k):
        return lax.dynamic_slice_in_dim(x, (index // 2 ^ k) * 2 * width, 2 * width, 1)

    lead = columns(conduction_orb, chips - 1)
    lead, conduction_orb = lax.optimization_barrier((lead, conduction_orb))
    far = [columns(conduction_orb, k) for k in range(half, chips - 1)] + [lead]
    far = [swap(far[k - half], 2 * k, size) for k in range(half, chips)]
    crossed = swap(valence_orb, 2 * half, size)
    crossed, conduction_orb = lax.optimization_barrier((crossed, conduction_orb))
    close = []
    for k in range(half):
        parts = [columns(conduction_orb, k), valence_orb, crossed] + [screened] * (k < near)
        close.append(jnp.concatenate(parts, axis=1))
    slabs = close[:1] + [swap(close[k], 2 * k, size) for k in range(1, half)] + far

    exc_t, *slabs = lax.optimization_barrier((exc_t, *slabs))
    other = swap(pack(place, slabs, width), 1, size)
    straight, cond, val = density_part(place, exc_t, slabs, chips)
    turned_in, cond_other, val_other = density_part(place, exc_t, [other], chips)
    density = jnp.concatenate([straight, turned_in], axis=1)

    densities = exchange(density, q_size, z_size, size)
    field = field_of(place, densities, slabs[:near], other, size, chips * (width + valence))
    field = lax.all_to_all(field, AXIS, split_axis=0, concat_axis=0, tiled=True)
    return project(place, field, [cond, cond_other], [val, val_other])


def body(size, excitations, valence_orb, conduction_orb, screened):
    powers = size >= 8 and size & (size - 1) == 0
    aligned = excitations.shape[1] % 128 == 0 and (2 * valence_orb.shape[0]) % 128 == 0
    run = body_slabs if powers and aligned else body_whole
    return run(size, excitations, valence_orb, conduction_orb, screened)


def solution(mesh):
    in_specs = (
        P("grp", "row", None),
        P(("grp", "row"), None),
        P(("grp", "row"), None),
        P(("grp", "row"), None),
    )
    out_specs = P("grp", "row", None)
    size = mesh.shape[AXIS]
    return jax.shard_map(
        functools.partial(body, size),
        mesh=mesh,
        in_specs=in_specs,
        out_specs=out_specs,
        check_vma=False,
    )
```

```python
import functools
import math

import jax
import jax.numpy as jnp
from jax import lax
from jax.experimental import pallas as pl
from jax.experimental.pallas import tpu as pltpu
from jax.sharding import PartitionSpec as P

AXIS = "row"
VMEM = pltpu.VMEM
NT = (((1,), (1,)), ((), ()))


def swap(x, bits, size):
    return lax.ppermute(x, AXIS, [(i, i ^ bits) for i in range(size)])


def exchange(x, step, count, size):
    return [x] + [swap(x, k * step, size) for k in range(1, count)]


def density_kernel(exc_ref, val_ref, cond_ref, out_ref):
    batch, valence, _ = exc_ref.shape
    cond, val = cond_ref[...], val_ref[...].astype(jnp.float32)
    group = math.gcd(batch, 4)
    sums = []
    for first in range(0, batch, group):
        exc = exc_ref[first : first + group].reshape(group * valence, -1)
        mixed = lax.dot_general(exc, cond, NT, preferred_element_type=jnp.float32)
        mixed = mixed.reshape(group, valence, -1) * val[None]
        sums.append(jnp.sum(mixed, axis=1))
    out_ref[...] = jnp.concatenate(sums, axis=0).astype(out_ref.dtype)


def partial_density(exc_t, val_t, cond_all):
    batch, valence, cond_local = exc_t.shape
    points = cond_all.shape[0]
    width = math.gcd(points, 1024)
    return pl.pallas_call(
        density_kernel,
        grid=(points // width,),
        in_specs=[
            pl.BlockSpec(memory_space=VMEM),
            pl.BlockSpec((valence, width), lambda i: (0, i)),
            pl.BlockSpec((width, cond_local), lambda i: (i, 0)),
        ],
        out_specs=pl.BlockSpec((batch, width), lambda i: (0, i)),
        out_shape=jax.ShapeDtypeStruct((batch, points), jnp.bfloat16),
        compiler_params=pltpu.CompilerParams(vmem_limit_bytes=16 << 20),
        cost_estimate=pl.CostEstimate(
            flops=2 * exc_t.size * points,
            bytes_accessed=2 * (exc_t.size + cond_all.size + val_t.size),
            transcendentals=0,
        ),
    )(exc_t, val_t, cond_all)


def action_kernel(z_ref, cond_ref, val_ref, *refs, layers, span):
    fields, (out_ref, held_ref, total_ref, sems) = refs[:layers], refs[layers:]
    batch = held_ref.shape[1]
    valence = val_ref.shape[0]
    for k, field in enumerate(fields):
        held_ref[z_ref[0] ^ k] = field[...].astype(jnp.float32)
    copies = []
    for first in range(0, batch, span):
        sides = []
        for b in range(first, first + span):
            row = jnp.concatenate([held_ref[k, b : b + 1, :] for k in range(layers)], axis=1)
            sides.append((val_ref[...].astype(jnp.float32) * row).astype(jnp.bfloat16))
        weights = jnp.concatenate(sides, axis=0)
        total = lax.dot_general(cond_ref[...], weights, NT, preferred_element_type=jnp.float32)
        for part in range(span):
            total_ref[first + part] = total[:, part * valence : (part + 1) * valence].astype(total_ref.dtype)
        piece = pl.ds(first, span)
        copies.append(pltpu.make_async_copy(total_ref.at[piece], out_ref.at[piece], sems.at[first // span]))
        copies[-1].start()
    for copy in copies:
        copy.wait()


def action_of(z, cond_t, val_t, fields):
    cond_local, points = cond_t.shape
    valence = val_t.shape[0]
    layers, (batch, chunk) = len(fields), fields[0].shape
    span = batch
    while span > 1 and span * valence * points * 2 > 1 << 20:
        span //= 2
    span = math.gcd(batch, span)
    whole = pl.BlockSpec(memory_space=VMEM)
    shape = (batch, cond_local, valence)
    return pl.pallas_call(
        functools.partial(action_kernel, layers=layers, span=span),
        in_specs=[pl.BlockSpec(memory_space=pltpu.SMEM)] + [whole] * (2 + layers),
        out_specs=pl.BlockSpec(memory_space=pl.ANY),
        out_shape=jax.ShapeDtypeStruct(shape, jnp.bfloat16),
        scratch_shapes=[
            pltpu.VMEM((layers, batch, chunk), jnp.float32),
            pltpu.VMEM(shape, jnp.bfloat16),
            pltpu.SemaphoreType.DMA((batch // span,)),
        ],
        compiler_params=pltpu.CompilerParams(vmem_limit_bytes=16 << 20),
        cost_estimate=pl.CostEstimate(
            flops=2 * batch * valence * cond_local * points,
            bytes_accessed=2 * (cond_t.size + val_t.size + batch * cond_local * valence),
            transcendentals=0,
        ),
    )(z, cond_t, val_t, *fields)


def body_whole(size, excitations, valence_orb, conduction_orb, screened):
    batch, cond_local, valence = excitations.shape
    rows = valence_orb.shape[0]
    points = rows * size
    q_size = 1 << ((size.bit_length() - 1) // 2)
    z_size = size // q_size
    index = lax.axis_index(AXIS)
    z, q = index // q_size, index % q_size

    blocks = conduction_orb.reshape(rows, size, cond_local).transpose(1, 0, 2)
    blocks, valence_orb, screened = lax.optimization_barrier((blocks, valence_orb, screened))
    cond_all = lax.all_to_all(blocks, AXIS, split_axis=0, concat_axis=0, tiled=True)
    cond_all = cond_all.reshape(points, cond_local)

    val = jnp.concatenate(exchange(valence_orb, q_size, z_size, size), axis=0)
    val = jnp.stack(exchange(val, 1, q_size, size)).reshape(size, rows, valence)
    val = jnp.concatenate(
        [val[((i % q_size) ^ q) * z_size + ((i // q_size) ^ z)] for i in range(size)], axis=0
    )
    val_t = val.T
    scr = jnp.stack(exchange(screened, 1, q_size, size))
    scr = jnp.concatenate([scr[k ^ q] for k in range(q_size)], axis=0)
    exc_t = excitations.transpose(0, 2, 1)

    density = partial_density(exc_t, val_t, cond_all)
    density = sum(d.astype(jnp.float32) for d in exchange(density, q_size, z_size, size))
    partial = lax.dot_general(
        density.astype(jnp.bfloat16), scr, NT, preferred_element_type=jnp.float32
    )
    sent = partial.astype(jnp.bfloat16)
    field = partial + sum(f.astype(jnp.float32) for f in exchange(sent, 1, q_size, size)[1:])
    fields = exchange(field.astype(jnp.bfloat16), q_size, z_size, size)
    return action_of(z.reshape(1), cond_all.T, val_t, fields)


def pack_kernel(index_ref, *refs, width):
    *slabs, near_ref, far_ref = refs
    half = len(slabs) // 2
    other = pl.ds(pl.multiple_of((1 - index_ref[0] % 2) * width, 128), width)
    valence = near_ref.shape[1] // half - width
    for k in range(half):
        near_ref[:, k * width : (k + 1) * width] = slabs[k][:, other]
        far_ref[:, k * width : (k + 1) * width] = slabs[half + k][:, other]
        at = half * width + k * valence
        near_ref[:, at : at + valence] = slabs[k][:, 2 * width : 2 * width + valence]
    at = half * width
    for slab in slabs[:half]:
        columns = slab.shape[1] - 2 * width - valence
        if columns:
            far_ref[:, at : at + columns] = slab[:, 2 * width + valence :]
            at += columns


def pack(index, slabs, width, valence):
    half, rows = len(slabs) // 2, slabs[0].shape[0]
    whole = pl.BlockSpec(memory_space=VMEM)
    extra = sum(slab.shape[1] - 2 * (width + valence) for slab in slabs[:half])
    columns = (half * (width + 2 * valence), half * width + extra)
    return pl.pallas_call(
        functools.partial(pack_kernel, width=width),
        in_specs=[pl.BlockSpec(memory_space=pltpu.SMEM)] + [whole] * len(slabs),
        out_specs=[whole] * 2,
        out_shape=[jax.ShapeDtypeStruct((rows, n), slabs[0].dtype) for n in columns],
        compiler_params=pltpu.CompilerParams(vmem_limit_bytes=8 << 20),
        cost_estimate=pl.CostEstimate(flops=0, bytes_accessed=1 << 20, transcendentals=0),
    )(index, *slabs)


def density_part_kernel(index_ref, *refs, straight):
    exc_ref, sources, (out_ref, cond_ref, val_ref) = refs[0], refs[1:-3], refs[-3:]
    batch, valence, width = exc_ref.shape
    rows = sources[0].shape[0]
    blocks = cond_ref.shape[0] // rows
    mine = pl.ds(pl.multiple_of(index_ref[0] % 2 * width, 128), width)
    val = []
    for k in range(blocks):
        if straight:
            half = blocks // 2
            cond = sources[k][:, mine]
            val_source, start = sources[k % half], 2 * width + k // half * valence
        else:
            cond = sources[-1][:, k * width : (k + 1) * width]
            val_source, start = sources[0], blocks * width + (2 * k + len(sources) - 1) * valence
        cond_ref[k * rows : (k + 1) * rows, :] = cond
        val.append(val_source[:, start : start + valence])
    val = jnp.concatenate(val, axis=0).T
    val_ref[...] = val
    val = val.astype(jnp.float32)
    part = math.gcd(batch, 4)
    sums = []
    for first in range(0, batch, part):
        exc = exc_ref[first : first + part].reshape(part * valence, width)
        mixed = lax.dot_general(exc, cond_ref[...], NT, preferred_element_type=jnp.float32)
        mixed = mixed.reshape(part, valence, -1) * val[None]
        sums.append(jnp.sum(mixed, axis=1))
    out_ref[...] = jnp.concatenate(sums, axis=0).astype(out_ref.dtype)


def density_part(index, exc_t, sources, blocks, straight):
    batch, valence, width = exc_t.shape
    points = blocks * sources[0].shape[0]
    whole = pl.BlockSpec(memory_space=VMEM)
    shapes = [(batch, points), (points, width), (valence, points)]
    return pl.pallas_call(
        functools.partial(density_part_kernel, straight=straight),
        in_specs=[pl.BlockSpec(memory_space=pltpu.SMEM)] + [whole] * (1 + len(sources)),
        out_specs=[whole] * len(shapes),
        out_shape=[jax.ShapeDtypeStruct(shape, jnp.bfloat16) for shape in shapes],
        compiler_params=pltpu.CompilerParams(vmem_limit_bytes=16 << 20),
        cost_estimate=pl.CostEstimate(
            flops=2 * exc_t.size * points, bytes_accessed=2 * exc_t.size, transcendentals=0
        ),
    )(index, exc_t, *sources)


def turned(x, flag):
    return jnp.where(flag, jnp.concatenate([x[:, x.shape[1] // 2 :], x[:, : x.shape[1] // 2]], axis=1), x)


def field_kernel(index_ref, *refs, z_size, near, start, rows):
    densities, screened, (forwarded, out_ref, held_ref) = refs[:z_size], refs[z_size:-3], refs[-3:]
    points = held_ref.shape[1]
    pair, chips = 2 * rows, points // (2 * rows)
    chip, core = index_ref[0] // 2, index_ref[0] % 2
    for k in range(chips):
        total = None
        for layer in range(z_size):
            at = (k ^ (layer * near)) * rows
            ref = densities[layer]
            halves = [ref[:, at + c * points // 2 : at + c * points // 2 + rows] for c in range(2)]
            term = jnp.concatenate(halves, axis=1).astype(jnp.float32)
            total = term if total is None else total + term
        place = pl.ds(pl.multiple_of((chip ^ k) * pair, pair), pair)
        held_ref[:, place] = turned(total, core == 1)
    density = held_ref[...].astype(jnp.bfloat16)
    for k in range(near):
        slab = screened[k]
        at = start + k * points
        both = [slab[:, slab.shape[1] - points :], forwarded[:, at : at + points]]
        both = jnp.concatenate(both, axis=0)
        partial = lax.dot_general(density, both, NT, preferred_element_type=jnp.float32)
        place = pl.ds(pl.multiple_of(((chip % near) ^ k) * pair, pair), pair)
        partial = turned(partial, core == 1).astype(out_ref.dtype)
        for target in range(out_ref.shape[0]):
            out_ref[target, :, place] = partial


def field_of(index, densities, screened, forwarded, copies, start):
    batch, points = densities[0].shape
    near, rows = len(screened), screened[0].shape[0]
    whole = pl.BlockSpec(memory_space=VMEM)
    columns = 2 * near * rows
    return pl.pallas_call(
        functools.partial(field_kernel, z_size=len(densities), near=near, start=start, rows=rows),
        in_specs=[pl.BlockSpec(memory_space=pltpu.SMEM)] + [whole] * (len(densities) + near + 1),
        out_specs=whole,
        out_shape=jax.ShapeDtypeStruct((copies, batch, columns), jnp.bfloat16),
        scratch_shapes=[pltpu.VMEM((batch, points), jnp.float32)],
        compiler_params=pltpu.CompilerParams(vmem_limit_bytes=16 << 20),
        cost_estimate=pl.CostEstimate(
            flops=2 * batch * points * columns, bytes_accessed=2 * points * columns, transcendentals=0
        ),
    )(index, *densities, *screened, forwarded)


def project_kernel(index_ref, field_ref, *refs, parts, span):
    conds, vals = refs[:parts], refs[parts : 2 * parts]
    out_ref, pairs_ref, total_ref, sems = refs[2 * parts :]
    size, batch, chunk = field_ref.shape
    chips, _, pair = pairs_ref.shape
    near = chunk // pair
    q_size = 2 * near
    valence = vals[0].shape[0]
    chip, core = index_ref[0] // 2, index_ref[0] % 2
    for layer in range(size // q_size):
        field = sum(field_ref[layer * q_size + k].astype(jnp.float32) for k in range(q_size))
        for k in range(near):
            pairs_ref[layer * near + k] = field[:, k * pair : (k + 1) * pair]
    both = [turned(pairs_ref[chip ^ k], core == 1) for k in range(chips)]
    halves = [x[:, : pair // 2] for x in both] + [x[:, pair // 2 :] for x in both]
    field = jnp.concatenate(halves, axis=1)
    field = field.astype(jnp.bfloat16).astype(jnp.float32)
    copies = []
    for first in range(0, batch, span):
        total, at = None, 0
        for cond, val in zip(conds, vals):
            stop = at + val.shape[1]
            sides = [
                (val[...].astype(jnp.float32) * field[b : b + 1, at:stop]).astype(jnp.bfloat16)
                for b in range(first, first + span)
            ]
            weights = jnp.concatenate(sides, axis=0)
            term = jnp.dot(weights, cond[...], preferred_element_type=jnp.float32)
            total, at = term if total is None else total + term, stop
        total = total.astype(total_ref.dtype)
        for part in range(span):
            b = first + part
            total_ref[b] = total[part * valence : (part + 1) * valence].T
            copies.append(pltpu.make_async_copy(total_ref.at[b], out_ref.at[b], sems.at[b]))
            copies[-1].start()
    for copy in copies:
        copy.wait()


def project(index, field, conds, vals):
    size, batch, _ = field.shape
    points, width = sum(cond.shape[0] for cond in conds), conds[0].shape[1]
    valence, span = vals[0].shape[0], math.gcd(batch, 4)
    whole = pl.BlockSpec(memory_space=VMEM)
    shape = (batch, width, valence)
    return pl.pallas_call(
        functools.partial(project_kernel, parts=len(conds), span=span),
        in_specs=[pl.BlockSpec(memory_space=pltpu.SMEM)] + [whole] * (1 + 2 * len(conds)),
        out_specs=pl.BlockSpec(memory_space=pl.ANY),
        out_shape=jax.ShapeDtypeStruct(shape, jnp.bfloat16),
        scratch_shapes=[
            pltpu.VMEM((size // 2, batch, 2 * points // size), jnp.float32),
            pltpu.VMEM(shape, jnp.bfloat16),
            pltpu.SemaphoreType.DMA((batch,)),
        ],
        compiler_params=pltpu.CompilerParams(vmem_limit_bytes=16 << 20),
        cost_estimate=pl.CostEstimate(
            flops=2 * batch * valence * width * points,
            bytes_accessed=2 * batch * width * valence,
            transcendentals=0,
        ),
    )(index, field, *conds, *vals)


def body_slabs(size, excitations, valence_orb, conduction_orb, screened):
    batch, width, valence = excitations.shape
    q_size = 1 << ((size.bit_length() - 1) // 2)
    z_size = size // q_size
    chips = size // 2
    index = lax.axis_index(AXIS)
    place = index.reshape(1)

    half, near = chips // 2, q_size // 2
    exc_t = excitations.transpose(0, 2, 1)

    def columns(x, k):
        return lax.dynamic_slice_in_dim(x, (index // 2 ^ k) * 2 * width, 2 * width, 1)

    lead = columns(conduction_orb, chips - 1)
    lead, conduction_orb = lax.optimization_barrier((lead, conduction_orb))
    far = [columns(conduction_orb, k) for k in range(half, chips - 1)] + [lead]
    far = [swap(far[k - half], 2 * k, size) for k in range(half, chips)]
    crossed = swap(valence_orb, 2 * half, size)
    crossed, conduction_orb = lax.optimization_barrier((crossed, conduction_orb))
    close = []
    for k in range(half):
        parts = [columns(conduction_orb, k), valence_orb, crossed] + [screened] * (k < near)
        close.append(jnp.concatenate(parts, axis=1))
    slabs = close[:1] + [swap(close[k], 2 * k, size) for k in range(1, half)] + far

    exc_t, *slabs = lax.optimization_barrier((exc_t, *slabs))
    near_part, far_part = pack(place, slabs, width, valence)
    near_part, far_part = swap(near_part, 1, size), swap(far_part, 1, size)
    parts = [
        density_part(place, exc_t, slabs, chips, True),
        density_part(place, exc_t, [near_part], half, False),
        density_part(place, exc_t, [near_part, far_part], half, False),
    ]
    density, conds, vals = [list(x) for x in zip(*parts)]
    density = jnp.concatenate(density, axis=1)

    densities = exchange(density, q_size, z_size, size)
    field = field_of(place, densities, slabs[:near], far_part, size, half * width)
    field = lax.all_to_all(field, AXIS, split_axis=0, concat_axis=0, tiled=True)
    return project(place, field, conds, vals)


def body(size, excitations, valence_orb, conduction_orb, screened):
    powers = size >= 8 and size & (size - 1) == 0
    aligned = excitations.shape[1] % 128 == 0 and (2 * valence_orb.shape[0]) % 128 == 0
    run = body_slabs if powers and aligned else body_whole
    return run(size, excitations, valence_orb, conduction_orb, screened)


def solution(mesh):
    in_specs = (
        P("grp", "row", None),
        P(("grp", "row"), None),
        P(("grp", "row"), None),
        P(("grp", "row"), None),
    )
    out_specs = P("grp", "row", None)
    size = mesh.shape[AXIS]
    return jax.shard_map(
        functools.partial(body, size),
        mesh=mesh,
        in_specs=in_specs,
        out_specs=out_specs,
        check_vma=False,
    )
```

```python
import functools
import math

import jax
import jax.numpy as jnp
from jax import lax
from jax.experimental import pallas as pl
from jax.experimental.pallas import tpu as pltpu
from jax.sharding import PartitionSpec as P

AXIS = "row"
VMEM = pltpu.VMEM
NT = (((1,), (1,)), ((), ()))


def swap(x, bits, size):
    return lax.ppermute(x, AXIS, [(i, i ^ bits) for i in range(size)])


def exchange(x, step, count, size):
    return [x] + [swap(x, k * step, size) for k in range(1, count)]


def density_kernel(exc_ref, val_ref, cond_ref, out_ref):
    batch, valence, _ = exc_ref.shape
    cond, val = cond_ref[...], val_ref[...].astype(jnp.float32)
    group = math.gcd(batch, 4)
    sums = []
    for first in range(0, batch, group):
        exc = exc_ref[first : first + group].reshape(group * valence, -1)
        mixed = lax.dot_general(exc, cond, NT, preferred_element_type=jnp.float32)
        mixed = mixed.reshape(group, valence, -1) * val[None]
        sums.append(jnp.sum(mixed, axis=1))
    out_ref[...] = jnp.concatenate(sums, axis=0).astype(out_ref.dtype)


def partial_density(exc_t, val_t, cond_all):
    batch, valence, cond_local = exc_t.shape
    points = cond_all.shape[0]
    width = math.gcd(points, 1024)
    return pl.pallas_call(
        density_kernel,
        grid=(points // width,),
        in_specs=[
            pl.BlockSpec(memory_space=VMEM),
            pl.BlockSpec((valence, width), lambda i: (0, i)),
            pl.BlockSpec((width, cond_local), lambda i: (i, 0)),
        ],
        out_specs=pl.BlockSpec((batch, width), lambda i: (0, i)),
        out_shape=jax.ShapeDtypeStruct((batch, points), jnp.bfloat16),
        compiler_params=pltpu.CompilerParams(vmem_limit_bytes=16 << 20),
        cost_estimate=pl.CostEstimate(
            flops=2 * exc_t.size * points,
            bytes_accessed=2 * (exc_t.size + cond_all.size + val_t.size),
            transcendentals=0,
        ),
    )(exc_t, val_t, cond_all)


def action_kernel(z_ref, cond_ref, val_ref, *refs, layers, span):
    fields, (out_ref, held_ref, total_ref, sems) = refs[:layers], refs[layers:]
    batch = held_ref.shape[1]
    valence = val_ref.shape[0]
    for k, field in enumerate(fields):
        held_ref[z_ref[0] ^ k] = field[...].astype(jnp.float32)
    copies = []
    for first in range(0, batch, span):
        sides = []
        for b in range(first, first + span):
            row = jnp.concatenate([held_ref[k, b : b + 1, :] for k in range(layers)], axis=1)
            sides.append((val_ref[...].astype(jnp.float32) * row).astype(jnp.bfloat16))
        weights = jnp.concatenate(sides, axis=0)
        total = lax.dot_general(cond_ref[...], weights, NT, preferred_element_type=jnp.float32)
        for part in range(span):
            total_ref[first + part] = total[:, part * valence : (part + 1) * valence].astype(total_ref.dtype)
        piece = pl.ds(first, span)
        copies.append(pltpu.make_async_copy(total_ref.at[piece], out_ref.at[piece], sems.at[first // span]))
        copies[-1].start()
    for copy in copies:
        copy.wait()


def action_of(z, cond_t, val_t, fields):
    cond_local, points = cond_t.shape
    valence = val_t.shape[0]
    layers, (batch, chunk) = len(fields), fields[0].shape
    span = batch
    while span > 1 and span * valence * points * 2 > 1 << 20:
        span //= 2
    span = math.gcd(batch, span)
    whole = pl.BlockSpec(memory_space=VMEM)
    shape = (batch, cond_local, valence)
    return pl.pallas_call(
        functools.partial(action_kernel, layers=layers, span=span),
        in_specs=[pl.BlockSpec(memory_space=pltpu.SMEM)] + [whole] * (2 + layers),
        out_specs=pl.BlockSpec(memory_space=pl.ANY),
        out_shape=jax.ShapeDtypeStruct(shape, jnp.bfloat16),
        scratch_shapes=[
            pltpu.VMEM((layers, batch, chunk), jnp.float32),
            pltpu.VMEM(shape, jnp.bfloat16),
            pltpu.SemaphoreType.DMA((batch // span,)),
        ],
        compiler_params=pltpu.CompilerParams(vmem_limit_bytes=16 << 20),
        cost_estimate=pl.CostEstimate(
            flops=2 * batch * valence * cond_local * points,
            bytes_accessed=2 * (cond_t.size + val_t.size + batch * cond_local * valence),
            transcendentals=0,
        ),
    )(z, cond_t, val_t, *fields)


def body_whole(size, excitations, valence_orb, conduction_orb, screened):
    batch, cond_local, valence = excitations.shape
    rows = valence_orb.shape[0]
    points = rows * size
    q_size = 1 << ((size.bit_length() - 1) // 2)
    z_size = size // q_size
    index = lax.axis_index(AXIS)
    z, q = index // q_size, index % q_size

    blocks = conduction_orb.reshape(rows, size, cond_local).transpose(1, 0, 2)
    blocks, valence_orb, screened = lax.optimization_barrier((blocks, valence_orb, screened))
    cond_all = lax.all_to_all(blocks, AXIS, split_axis=0, concat_axis=0, tiled=True)
    cond_all = cond_all.reshape(points, cond_local)

    val = jnp.concatenate(exchange(valence_orb, q_size, z_size, size), axis=0)
    val = jnp.stack(exchange(val, 1, q_size, size)).reshape(size, rows, valence)
    val = jnp.concatenate(
        [val[((i % q_size) ^ q) * z_size + ((i // q_size) ^ z)] for i in range(size)], axis=0
    )
    val_t = val.T
    scr = jnp.stack(exchange(screened, 1, q_size, size))
    scr = jnp.concatenate([scr[k ^ q] for k in range(q_size)], axis=0)
    exc_t = excitations.transpose(0, 2, 1)

    density = partial_density(exc_t, val_t, cond_all)
    density = sum(d.astype(jnp.float32) for d in exchange(density, q_size, z_size, size))
    partial = lax.dot_general(
        density.astype(jnp.bfloat16), scr, NT, preferred_element_type=jnp.float32
    )
    sent = partial.astype(jnp.bfloat16)
    field = partial + sum(f.astype(jnp.float32) for f in exchange(sent, 1, q_size, size)[1:])
    fields = exchange(field.astype(jnp.bfloat16), q_size, z_size, size)
    return action_of(z.reshape(1), cond_all.T, val_t, fields)


def pack_kernel(index_ref, *refs, width):
    *slabs, near_ref, far_ref = refs
    half = len(slabs) // 2
    other = pl.ds(pl.multiple_of((1 - index_ref[0] % 2) * width, 128), width)
    valence = near_ref.shape[1] // half - width
    for k in range(half):
        near_ref[:, k * width : (k + 1) * width] = slabs[k][:, other]
        far_ref[:, k * width : (k + 1) * width] = slabs[half + k][:, other]
        at = half * width + k * valence
        near_ref[:, at : at + valence] = slabs[k][:, 2 * width : 2 * width + valence]
    at = half * width
    for slab in slabs[:half]:
        columns = slab.shape[1] - 2 * width - valence
        if columns:
            far_ref[:, at : at + columns] = slab[:, 2 * width + valence :]
            at += columns


def pack(index, slabs, width, valence):
    half, rows = len(slabs) // 2, slabs[0].shape[0]
    whole = pl.BlockSpec(memory_space=VMEM)
    extra = sum(slab.shape[1] - 2 * (width + valence) for slab in slabs[:half])
    columns = (half * (width + 2 * valence), half * width + extra)
    return pl.pallas_call(
        functools.partial(pack_kernel, width=width),
        in_specs=[pl.BlockSpec(memory_space=pltpu.SMEM)] + [whole] * len(slabs),
        out_specs=[whole] * 2,
        out_shape=[jax.ShapeDtypeStruct((rows, n), slabs[0].dtype) for n in columns],
        compiler_params=pltpu.CompilerParams(vmem_limit_bytes=8 << 20),
        cost_estimate=pl.CostEstimate(flops=0, bytes_accessed=1 << 20, transcendentals=0),
    )(index, *slabs)


def density_part_kernel(index_ref, *refs, straight):
    exc_ref, sources, (out_ref, cond_ref, val_ref) = refs[0], refs[1:-3], refs[-3:]
    batch, valence, width = exc_ref.shape
    rows = sources[0].shape[0]
    blocks = cond_ref.shape[0] // rows
    mine = pl.ds(pl.multiple_of(index_ref[0] % 2 * width, 128), width)
    val = []
    for k in range(blocks):
        if straight:
            half = blocks // 2
            cond = sources[k][:, mine]
            val_source, start = sources[k % half], 2 * width + k // half * valence
        else:
            cond = sources[-1][:, k * width : (k + 1) * width]
            val_source, start = sources[0], blocks * width + (2 * k + len(sources) - 1) * valence
        cond_ref[k * rows : (k + 1) * rows, :] = cond
        val.append(val_source[:, start : start + valence])
    val = jnp.concatenate(val, axis=0).T
    val_ref[...] = val
    val = val.astype(jnp.float32)
    part = math.gcd(batch, 4)
    sums = []
    for first in range(0, batch, part):
        exc = exc_ref[first : first + part].reshape(part * valence, width)
        mixed = lax.dot_general(exc, cond_ref[...], NT, preferred_element_type=jnp.float32)
        mixed = mixed.reshape(part, valence, -1) * val[None]
        sums.append(jnp.sum(mixed, axis=1))
    out_ref[...] = jnp.concatenate(sums, axis=0).astype(out_ref.dtype)


def density_part(index, exc_t, sources, blocks, straight):
    batch, valence, width = exc_t.shape
    points = blocks * sources[0].shape[0]
    whole = pl.BlockSpec(memory_space=VMEM)
    shapes = [(batch, points), (points, width), (valence, points)]
    return pl.pallas_call(
        functools.partial(density_part_kernel, straight=straight),
        in_specs=[pl.BlockSpec(memory_space=pltpu.SMEM)] + [whole] * (1 + len(sources)),
        out_specs=[whole] * len(shapes),
        out_shape=[jax.ShapeDtypeStruct(shape, jnp.bfloat16) for shape in shapes],
        compiler_params=pltpu.CompilerParams(vmem_limit_bytes=16 << 20),
        cost_estimate=pl.CostEstimate(
            flops=2 * exc_t.size * points, bytes_accessed=2 * exc_t.size, transcendentals=0
        ),
    )(index, exc_t, *sources)


def turned(x, flag):
    return jnp.where(flag, jnp.concatenate([x[:, x.shape[1] // 2 :], x[:, : x.shape[1] // 2]], axis=1), x)


def field_kernel(index_ref, *refs, z_size, near, start, rows):
    densities, screened, (forwarded, out_ref, held_ref) = refs[:z_size], refs[z_size:-3], refs[-3:]
    points = held_ref.shape[1]
    pair, chips = 2 * rows, points // (2 * rows)
    chip, core = index_ref[0] // 2, index_ref[0] % 2
    for k in range(chips):
        total = None
        for layer in range(z_size):
            at = (k ^ (layer * near)) * rows
            ref = densities[layer]
            halves = [ref[:, at + c * points // 2 : at + c * points // 2 + rows] for c in range(2)]
            term = jnp.concatenate(halves, axis=1).astype(jnp.float32)
            total = term if total is None else total + term
        place = pl.ds(pl.multiple_of((chip ^ k) * pair, pair), pair)
        held_ref[:, place] = turned(total, core == 1)
    total = held_ref[...]
    high = total.astype(jnp.bfloat16)
    low = (total - high.astype(jnp.float32)).astype(jnp.bfloat16)
    density = jnp.concatenate([high, low], axis=0)
    batch = high.shape[0]
    for k in range(near):
        slab = screened[k]
        at = start + k * points
        both = [slab[:, slab.shape[1] - points :], forwarded[:, at : at + points]]
        both = jnp.concatenate(both, axis=0)
        partial = lax.dot_general(density, both, NT, preferred_element_type=jnp.float32)
        partial = partial[:batch] + partial[batch:]
        place = pl.ds(pl.multiple_of(((chip % near) ^ k) * pair, pair), pair)
        partial = turned(partial, core == 1).astype(out_ref.dtype)
        for target in range(out_ref.shape[0]):
            out_ref[target, :, place] = partial


def field_of(index, densities, screened, forwarded, copies, start):
    batch, points = densities[0].shape
    near, rows = len(screened), screened[0].shape[0]
    whole = pl.BlockSpec(memory_space=VMEM)
    columns = 2 * near * rows
    return pl.pallas_call(
        functools.partial(field_kernel, z_size=len(densities), near=near, start=start, rows=rows),
        in_specs=[pl.BlockSpec(memory_space=pltpu.SMEM)] + [whole] * (len(densities) + near + 1),
        out_specs=whole,
        out_shape=jax.ShapeDtypeStruct((copies, batch, columns), jnp.bfloat16),
        scratch_shapes=[pltpu.VMEM((batch, points), jnp.float32)],
        compiler_params=pltpu.CompilerParams(vmem_limit_bytes=16 << 20),
        cost_estimate=pl.CostEstimate(
            flops=2 * batch * points * columns, bytes_accessed=2 * points * columns, transcendentals=0
        ),
    )(index, *densities, *screened, forwarded)


def project_kernel(index_ref, field_ref, *refs, parts, span):
    conds, vals = refs[:parts], refs[parts : 2 * parts]
    out_ref, pairs_ref, total_ref, sems = refs[2 * parts :]
    size, batch, chunk = field_ref.shape
    chips, _, pair = pairs_ref.shape
    near = chunk // pair
    q_size = 2 * near
    valence = vals[0].shape[0]
    chip, core = index_ref[0] // 2, index_ref[0] % 2
    for layer in range(size // q_size):
        field = sum(field_ref[layer * q_size + k].astype(jnp.float32) for k in range(q_size))
        for k in range(near):
            pairs_ref[layer * near + k] = field[:, k * pair : (k + 1) * pair]
    both = [turned(pairs_ref[chip ^ k], core == 1) for k in range(chips)]
    halves = [x[:, : pair // 2] for x in both] + [x[:, pair // 2 :] for x in both]
    field = jnp.concatenate(halves, axis=1)
    field = field.astype(jnp.bfloat16).astype(jnp.float32)
    copies = []
    for first in range(0, batch, span):
        total, at = None, 0
        for cond, val in zip(conds, vals):
            stop = at + val.shape[1]
            sides = [
                (val[...].astype(jnp.float32) * field[b : b + 1, at:stop]).astype(jnp.bfloat16)
                for b in range(first, first + span)
            ]
            weights = jnp.concatenate(sides, axis=0)
            term = jnp.dot(weights, cond[...], preferred_element_type=jnp.float32)
            total, at = term if total is None else total + term, stop
        total = total.astype(total_ref.dtype)
        for part in range(span):
            b = first + part
            total_ref[b] = total[part * valence : (part + 1) * valence].T
            copies.append(pltpu.make_async_copy(total_ref.at[b], out_ref.at[b], sems.at[b]))
            copies[-1].start()
    for copy in copies:
        copy.wait()


def project(index, field, conds, vals):
    size, batch, _ = field.shape
    points, width = sum(cond.shape[0] for cond in conds), conds[0].shape[1]
    valence, span = vals[0].shape[0], math.gcd(batch, 4)
    whole = pl.BlockSpec(memory_space=VMEM)
    shape = (batch, width, valence)
    return pl.pallas_call(
        functools.partial(project_kernel, parts=len(conds), span=span),
        in_specs=[pl.BlockSpec(memory_space=pltpu.SMEM)] + [whole] * (1 + 2 * len(conds)),
        out_specs=pl.BlockSpec(memory_space=pl.ANY),
        out_shape=jax.ShapeDtypeStruct(shape, jnp.bfloat16),
        scratch_shapes=[
            pltpu.VMEM((size // 2, batch, 2 * points // size), jnp.float32),
            pltpu.VMEM(shape, jnp.bfloat16),
            pltpu.SemaphoreType.DMA((batch,)),
        ],
        compiler_params=pltpu.CompilerParams(vmem_limit_bytes=16 << 20),
        cost_estimate=pl.CostEstimate(
            flops=2 * batch * valence * width * points,
            bytes_accessed=2 * batch * width * valence,
            transcendentals=0,
        ),
    )(index, field, *conds, *vals)


def body_slabs(size, excitations, valence_orb, conduction_orb, screened):
    batch, width, valence = excitations.shape
    q_size = 1 << ((size.bit_length() - 1) // 2)
    z_size = size // q_size
    chips = size // 2
    index = lax.axis_index(AXIS)
    place = index.reshape(1)

    half, near = chips // 2, q_size // 2
    exc_t = excitations.transpose(0, 2, 1)

    def columns(x, k):
        return lax.dynamic_slice_in_dim(x, (index // 2 ^ k) * 2 * width, 2 * width, 1)

    lead = columns(conduction_orb, chips - 1)
    lead, conduction_orb = lax.optimization_barrier((lead, conduction_orb))
    far = [columns(conduction_orb, k) for k in range(half, chips - 1)] + [lead]
    far = [swap(far[k - half], 2 * k, size) for k in range(half, chips)]
    crossed = swap(valence_orb, 2 * half, size)
    crossed, conduction_orb = lax.optimization_barrier((crossed, conduction_orb))
    close = []
    for k in range(half):
        parts = [columns(conduction_orb, k), valence_orb, crossed] + [screened] * (k < near)
        close.append(jnp.concatenate(parts, axis=1))
    slabs = close[:1] + [swap(close[k], 2 * k, size) for k in range(1, half)] + far

    exc_t, *slabs = lax.optimization_barrier((exc_t, *slabs))
    near_part, far_part = pack(place, slabs, width, valence)
    near_part, far_part = swap(near_part, 1, size), swap(far_part, 1, size)
    parts = [
        density_part(place, exc_t, slabs, chips, True),
        density_part(place, exc_t, [near_part], half, False),
        density_part(place, exc_t, [near_part, far_part], half, False),
    ]
    density, conds, vals = [list(x) for x in zip(*parts)]
    density = jnp.concatenate(density, axis=1)

    densities = exchange(density, q_size, z_size, size)
    field = field_of(place, densities, slabs[:near], far_part, size, half * width)
    field = lax.all_to_all(field, AXIS, split_axis=0, concat_axis=0, tiled=True)
    return project(place, field, conds, vals)


def body(size, excitations, valence_orb, conduction_orb, screened):
    powers = size >= 8 and size & (size - 1) == 0
    aligned = excitations.shape[1] % 128 == 0 and (2 * valence_orb.shape[0]) % 128 == 0
    run = body_slabs if powers and aligned else body_whole
    return run(size, excitations, valence_orb, conduction_orb, screened)


def solution(mesh):
    in_specs = (
        P("grp", "row", None),
        P(("grp", "row"), None),
        P(("grp", "row"), None),
        P(("grp", "row"), None),
    )
    out_specs = P("grp", "row", None)
    size = mesh.shape[AXIS]
    return jax.shard_map(
        functools.partial(body, size),
        mesh=mesh,
        in_specs=in_specs,
        out_specs=out_specs,
        check_vma=False,
    )
```

```python
import functools
import math

import jax
import jax.numpy as jnp
from jax import lax
from jax.experimental import pallas as pl
from jax.experimental.pallas import tpu as pltpu
from jax.sharding import PartitionSpec as P

AXIS = "row"
VMEM = pltpu.VMEM
NT = (((1,), (1,)), ((), ()))


def swap(x, bits, size):
    return lax.ppermute(x, AXIS, [(i, i ^ bits) for i in range(size)])


def exchange(x, step, count, size):
    return [x] + [swap(x, k * step, size) for k in range(1, count)]


def density_kernel(exc_ref, val_ref, cond_ref, out_ref):
    batch, valence, _ = exc_ref.shape
    cond, val = cond_ref[...], val_ref[...].astype(jnp.float32)
    group = math.gcd(batch, 4)
    sums = []
    for first in range(0, batch, group):
        exc = exc_ref[first : first + group].reshape(group * valence, -1)
        mixed = lax.dot_general(exc, cond, NT, preferred_element_type=jnp.float32)
        mixed = mixed.reshape(group, valence, -1) * val[None]
        sums.append(jnp.sum(mixed, axis=1))
    out_ref[...] = jnp.concatenate(sums, axis=0).astype(out_ref.dtype)


def partial_density(exc_t, val_t, cond_all):
    batch, valence, cond_local = exc_t.shape
    points = cond_all.shape[0]
    width = math.gcd(points, 1024)
    return pl.pallas_call(
        density_kernel,
        grid=(points // width,),
        in_specs=[
            pl.BlockSpec(memory_space=VMEM),
            pl.BlockSpec((valence, width), lambda i: (0, i)),
            pl.BlockSpec((width, cond_local), lambda i: (i, 0)),
        ],
        out_specs=pl.BlockSpec((batch, width), lambda i: (0, i)),
        out_shape=jax.ShapeDtypeStruct((batch, points), jnp.bfloat16),
        compiler_params=pltpu.CompilerParams(vmem_limit_bytes=16 << 20),
        cost_estimate=pl.CostEstimate(
            flops=2 * exc_t.size * points,
            bytes_accessed=2 * (exc_t.size + cond_all.size + val_t.size),
            transcendentals=0,
        ),
    )(exc_t, val_t, cond_all)


def action_kernel(z_ref, cond_ref, val_ref, *refs, layers, span):
    fields, (out_ref, held_ref, total_ref, sems) = refs[:layers], refs[layers:]
    batch = held_ref.shape[1]
    valence = val_ref.shape[0]
    for k, field in enumerate(fields):
        held_ref[z_ref[0] ^ k] = field[...].astype(jnp.float32)
    copies = []
    for first in range(0, batch, span):
        sides = []
        for b in range(first, first + span):
            row = jnp.concatenate([held_ref[k, b : b + 1, :] for k in range(layers)], axis=1)
            sides.append((val_ref[...].astype(jnp.float32) * row).astype(jnp.bfloat16))
        weights = jnp.concatenate(sides, axis=0)
        total = lax.dot_general(cond_ref[...], weights, NT, preferred_element_type=jnp.float32)
        for part in range(span):
            total_ref[first + part] = total[:, part * valence : (part + 1) * valence].astype(total_ref.dtype)
        piece = pl.ds(first, span)
        copies.append(pltpu.make_async_copy(total_ref.at[piece], out_ref.at[piece], sems.at[first // span]))
        copies[-1].start()
    for copy in copies:
        copy.wait()


def action_of(z, cond_t, val_t, fields):
    cond_local, points = cond_t.shape
    valence = val_t.shape[0]
    layers, (batch, chunk) = len(fields), fields[0].shape
    span = batch
    while span > 1 and span * valence * points * 2 > 1 << 20:
        span //= 2
    span = math.gcd(batch, span)
    whole = pl.BlockSpec(memory_space=VMEM)
    shape = (batch, cond_local, valence)
    return pl.pallas_call(
        functools.partial(action_kernel, layers=layers, span=span),
        in_specs=[pl.BlockSpec(memory_space=pltpu.SMEM)] + [whole] * (2 + layers),
        out_specs=pl.BlockSpec(memory_space=pl.ANY),
        out_shape=jax.ShapeDtypeStruct(shape, jnp.bfloat16),
        scratch_shapes=[
            pltpu.VMEM((layers, batch, chunk), jnp.float32),
            pltpu.VMEM(shape, jnp.bfloat16),
            pltpu.SemaphoreType.DMA((batch // span,)),
        ],
        compiler_params=pltpu.CompilerParams(vmem_limit_bytes=16 << 20),
        cost_estimate=pl.CostEstimate(
            flops=2 * batch * valence * cond_local * points,
            bytes_accessed=2 * (cond_t.size + val_t.size + batch * cond_local * valence),
            transcendentals=0,
        ),
    )(z, cond_t, val_t, *fields)


def body_whole(size, excitations, valence_orb, conduction_orb, screened):
    batch, cond_local, valence = excitations.shape
    rows = valence_orb.shape[0]
    points = rows * size
    q_size = 1 << ((size.bit_length() - 1) // 2)
    z_size = size // q_size
    index = lax.axis_index(AXIS)
    z, q = index // q_size, index % q_size

    blocks = conduction_orb.reshape(rows, size, cond_local).transpose(1, 0, 2)
    blocks, valence_orb, screened = lax.optimization_barrier((blocks, valence_orb, screened))
    cond_all = lax.all_to_all(blocks, AXIS, split_axis=0, concat_axis=0, tiled=True)
    cond_all = cond_all.reshape(points, cond_local)

    val = jnp.concatenate(exchange(valence_orb, q_size, z_size, size), axis=0)
    val = jnp.stack(exchange(val, 1, q_size, size)).reshape(size, rows, valence)
    val = jnp.concatenate(
        [val[((i % q_size) ^ q) * z_size + ((i // q_size) ^ z)] for i in range(size)], axis=0
    )
    val_t = val.T
    scr = jnp.stack(exchange(screened, 1, q_size, size))
    scr = jnp.concatenate([scr[k ^ q] for k in range(q_size)], axis=0)
    exc_t = excitations.transpose(0, 2, 1)

    density = partial_density(exc_t, val_t, cond_all)
    density = sum(d.astype(jnp.float32) for d in exchange(density, q_size, z_size, size))
    partial = lax.dot_general(
        density.astype(jnp.bfloat16), scr, NT, preferred_element_type=jnp.float32
    )
    sent = partial.astype(jnp.bfloat16)
    field = partial + sum(f.astype(jnp.float32) for f in exchange(sent, 1, q_size, size)[1:])
    fields = exchange(field.astype(jnp.bfloat16), q_size, z_size, size)
    return action_of(z.reshape(1), cond_all.T, val_t, fields)


def pack_kernel(index_ref, *refs, width):
    *slabs, near_ref, far_ref = refs
    half = len(slabs) // 2
    other = pl.ds(pl.multiple_of((1 - index_ref[0] % 2) * width, 128), width)
    valence = near_ref.shape[1] // half - width
    for k in range(half):
        near_ref[:, k * width : (k + 1) * width] = slabs[k][:, other]
        far_ref[:, k * width : (k + 1) * width] = slabs[half + k][:, other]
        at = half * width + k * valence
        near_ref[:, at : at + valence] = slabs[k][:, 2 * width : 2 * width + valence]
    at = half * width
    for slab in slabs[:half]:
        columns = slab.shape[1] - 2 * width - valence
        if columns:
            far_ref[:, at : at + columns] = slab[:, 2 * width + valence :]
            at += columns


def pack(index, slabs, width, valence):
    half, rows = len(slabs) // 2, slabs[0].shape[0]
    whole = pl.BlockSpec(memory_space=VMEM)
    extra = sum(slab.shape[1] - 2 * (width + valence) for slab in slabs[:half])
    columns = (half * (width + 2 * valence), half * width + extra)
    return pl.pallas_call(
        functools.partial(pack_kernel, width=width),
        in_specs=[pl.BlockSpec(memory_space=pltpu.SMEM)] + [whole] * len(slabs),
        out_specs=[whole] * 2,
        out_shape=[jax.ShapeDtypeStruct((rows, n), slabs[0].dtype) for n in columns],
        compiler_params=pltpu.CompilerParams(vmem_limit_bytes=8 << 20),
        cost_estimate=pl.CostEstimate(flops=0, bytes_accessed=1 << 20, transcendentals=0),
    )(index, *slabs)


def density_part_kernel(index_ref, *refs, straight):
    exc_ref, sources, (out_ref, cond_ref, val_ref) = refs[0], refs[1:-3], refs[-3:]
    batch, valence, width = exc_ref.shape
    rows = sources[0].shape[0]
    blocks = cond_ref.shape[0] // rows
    mine = pl.ds(pl.multiple_of(index_ref[0] % 2 * width, 128), width)
    val = []
    for k in range(blocks):
        if straight:
            half = blocks // 2
            cond = sources[k][:, mine]
            val_source, start = sources[k % half], 2 * width + k // half * valence
        else:
            cond = sources[-1][:, k * width : (k + 1) * width]
            val_source, start = sources[0], blocks * width + (2 * k + len(sources) - 1) * valence
        cond_ref[k * rows : (k + 1) * rows, :] = cond
        val.append(val_source[:, start : start + valence])
    val = jnp.concatenate(val, axis=0).T
    val_ref[...] = val
    val = val.astype(jnp.float32)
    part = math.gcd(batch, 4)
    sums = []
    for first in range(0, batch, part):
        exc = exc_ref[first : first + part].reshape(part * valence, width)
        mixed = lax.dot_general(exc, cond_ref[...], NT, preferred_element_type=jnp.float32)
        mixed = mixed.reshape(part, valence, -1) * val[None]
        sums.append(jnp.sum(mixed, axis=1))
    out_ref[...] = jnp.concatenate(sums, axis=0).astype(out_ref.dtype)


def density_part(index, exc_t, sources, blocks, straight):
    batch, valence, width = exc_t.shape
    points = blocks * sources[0].shape[0]
    whole = pl.BlockSpec(memory_space=VMEM)
    shapes = [(batch, points), (points, width), (valence, points)]
    return pl.pallas_call(
        functools.partial(density_part_kernel, straight=straight),
        in_specs=[pl.BlockSpec(memory_space=pltpu.SMEM)] + [whole] * (1 + len(sources)),
        out_specs=[whole] * len(shapes),
        out_shape=[jax.ShapeDtypeStruct(shape, jnp.bfloat16) for shape in shapes],
        compiler_params=pltpu.CompilerParams(vmem_limit_bytes=16 << 20),
        cost_estimate=pl.CostEstimate(
            flops=2 * exc_t.size * points, bytes_accessed=2 * exc_t.size, transcendentals=0
        ),
    )(index, exc_t, *sources)


def turned(x, flag):
    return jnp.where(flag, jnp.concatenate([x[:, x.shape[1] // 2 :], x[:, : x.shape[1] // 2]], axis=1), x)


def field_kernel(index_ref, *refs, z_size, near, start, rows):
    densities, screened, (forwarded, out_ref, held_ref) = refs[:z_size], refs[z_size:-3], refs[-3:]
    points = held_ref.shape[1]
    pair, chips = 2 * rows, points // (2 * rows)
    chip, core = index_ref[0] // 2, index_ref[0] % 2
    for k in range(chips):
        total = None
        for layer in range(z_size):
            at = (k ^ (layer * near)) * rows
            ref = densities[layer]
            halves = [ref[:, at + c * points // 2 : at + c * points // 2 + rows] for c in range(2)]
            term = jnp.concatenate(halves, axis=1).astype(jnp.float32)
            total = term if total is None else total + term
        place = pl.ds(pl.multiple_of((chip ^ k) * pair, pair), pair)
        held_ref[:, place] = turned(total, core == 1)
    total = held_ref[...]
    high = total.astype(jnp.bfloat16)
    low = (total - high.astype(jnp.float32)).astype(jnp.bfloat16)
    density = jnp.concatenate([high, low], axis=0)
    batch = high.shape[0]
    for k in range(near):
        slab = screened[k]
        at = start + k * points
        both = [slab[:, slab.shape[1] - points :], forwarded[:, at : at + points]]
        both = jnp.concatenate(both, axis=0)
        partial = lax.dot_general(density, both, NT, preferred_element_type=jnp.float32)
        partial = partial[:batch] + partial[batch:]
        place = pl.ds(pl.multiple_of(((chip % near) ^ k) * pair, pair), pair)
        out_ref[:, place] = turned(partial, core == 1).astype(out_ref.dtype)


def field_of(index, densities, screened, forwarded, start):
    batch, points = densities[0].shape
    near, rows = len(screened), screened[0].shape[0]
    whole = pl.BlockSpec(memory_space=VMEM)
    columns = 2 * near * rows
    return pl.pallas_call(
        functools.partial(field_kernel, z_size=len(densities), near=near, start=start, rows=rows),
        in_specs=[pl.BlockSpec(memory_space=pltpu.SMEM)] + [whole] * (len(densities) + near + 1),
        out_specs=whole,
        out_shape=jax.ShapeDtypeStruct((batch, columns), jnp.bfloat16),
        scratch_shapes=[pltpu.VMEM((batch, points), jnp.float32)],
        compiler_params=pltpu.CompilerParams(vmem_limit_bytes=16 << 20),
        cost_estimate=pl.CostEstimate(
            flops=2 * batch * points * columns, bytes_accessed=2 * points * columns, transcendentals=0
        ),
    )(index, *densities, *screened, forwarded)


def project_kernel(index_ref, *refs, layers, parts, span):
    fields, refs = refs[:layers], refs[layers:]
    conds, vals = refs[:parts], refs[parts : 2 * parts]
    out_ref, pairs_ref, total_ref, sems = refs[2 * parts :]
    batch, chunk = fields[0].shape
    chips, _, pair = pairs_ref.shape
    near, valence = chunk // pair, vals[0].shape[0]
    chip, core = index_ref[0] // 2, index_ref[0] % 2
    for layer, ref in enumerate(fields):
        for k in range(near):
            pairs_ref[(chip // near ^ layer) * near + k] = ref[:, k * pair : (k + 1) * pair].astype(jnp.float32)
    both = [turned(pairs_ref[chip ^ k], core == 1) for k in range(chips)]
    halves = [x[:, : pair // 2] for x in both] + [x[:, pair // 2 :] for x in both]
    field = jnp.concatenate(halves, axis=1)
    field = field.astype(jnp.bfloat16).astype(jnp.float32)
    copies = []
    for first in range(0, batch, span):
        total, at = None, 0
        for cond, val in zip(conds, vals):
            stop = at + val.shape[1]
            sides = [
                (val[...].astype(jnp.float32) * field[b : b + 1, at:stop]).astype(jnp.bfloat16)
                for b in range(first, first + span)
            ]
            weights = jnp.concatenate(sides, axis=0)
            term = jnp.dot(weights, cond[...], preferred_element_type=jnp.float32)
            total, at = term if total is None else total + term, stop
        total = total.astype(total_ref.dtype)
        for part in range(span):
            b = first + part
            total_ref[b] = total[part * valence : (part + 1) * valence].T
            copies.append(pltpu.make_async_copy(total_ref.at[b], out_ref.at[b], sems.at[b]))
            copies[-1].start()
    for copy in copies:
        copy.wait()


def project(index, fields, conds, vals, size):
    batch = fields[0].shape[0]
    points, width = sum(cond.shape[0] for cond in conds), conds[0].shape[1]
    valence, span = vals[0].shape[0], math.gcd(batch, 4)
    whole = pl.BlockSpec(memory_space=VMEM)
    shape = (batch, width, valence)
    return pl.pallas_call(
        functools.partial(project_kernel, layers=len(fields), parts=len(conds), span=span),
        in_specs=[pl.BlockSpec(memory_space=pltpu.SMEM)] + [whole] * (len(fields) + 2 * len(conds)),
        out_specs=pl.BlockSpec(memory_space=pl.ANY),
        out_shape=jax.ShapeDtypeStruct(shape, jnp.bfloat16),
        scratch_shapes=[
            pltpu.VMEM((size // 2, batch, 2 * points // size), jnp.float32),
            pltpu.VMEM(shape, jnp.bfloat16),
            pltpu.SemaphoreType.DMA((batch,)),
        ],
        compiler_params=pltpu.CompilerParams(vmem_limit_bytes=16 << 20),
        cost_estimate=pl.CostEstimate(
            flops=2 * batch * valence * width * points,
            bytes_accessed=2 * batch * width * valence,
            transcendentals=0,
        ),
    )(index, *fields, *conds, *vals)


def body_slabs(size, excitations, valence_orb, conduction_orb, screened):
    batch, width, valence = excitations.shape
    q_size = 1 << ((size.bit_length() - 1) // 2)
    z_size = size // q_size
    chips = size // 2
    index = lax.axis_index(AXIS)
    place = index.reshape(1)

    half, near = chips // 2, q_size // 2
    exc_t = excitations.transpose(0, 2, 1)

    def columns(x, k):
        return lax.dynamic_slice_in_dim(x, (index // 2 ^ k) * 2 * width, 2 * width, 1)

    lead = columns(conduction_orb, chips - 1)
    lead, conduction_orb = lax.optimization_barrier((lead, conduction_orb))
    far = [columns(conduction_orb, k) for k in range(half, chips - 1)] + [lead]
    far = [swap(far[k - half], 2 * k, size) for k in range(half, chips)]
    crossed = swap(valence_orb, 2 * half, size)
    crossed, conduction_orb = lax.optimization_barrier((crossed, conduction_orb))
    close = []
    for k in range(half):
        parts = [columns(conduction_orb, k), valence_orb, crossed] + [screened] * (k < near)
        close.append(jnp.concatenate(parts, axis=1))
    slabs = close[:1] + [swap(close[k], 2 * k, size) for k in range(1, half)] + far

    exc_t, *slabs = lax.optimization_barrier((exc_t, *slabs))
    near_part, far_part = pack(place, slabs, width, valence)
    near_part, far_part = swap(near_part, 1, size), swap(far_part, 1, size)
    parts = [
        density_part(place, exc_t, slabs, chips, True),
        density_part(place, exc_t, [near_part], half, False),
        density_part(place, exc_t, [near_part, far_part], half, False),
    ]
    density, conds, vals = [list(x) for x in zip(*parts)]
    density = jnp.concatenate(density, axis=1)

    densities = exchange(density, q_size, z_size, size)
    partial = field_of(place, densities, slabs[:near], far_part, half * width)
    field = sum(x.astype(jnp.float32) for x in exchange(partial, 1, q_size, size)).astype(jnp.bfloat16)
    return project(place, exchange(field, q_size, z_size, size), conds, vals, size)


def body(size, excitations, valence_orb, conduction_orb, screened):
    powers = size >= 8 and size & (size - 1) == 0
    aligned = excitations.shape[1] % 128 == 0 and (2 * valence_orb.shape[0]) % 128 == 0
    run = body_slabs if powers and aligned else body_whole
    return run(size, excitations, valence_orb, conduction_orb, screened)


def solution(mesh):
    in_specs = (
        P("grp", "row", None),
        P(("grp", "row"), None),
        P(("grp", "row"), None),
        P(("grp", "row"), None),
    )
    out_specs = P("grp", "row", None)
    size = mesh.shape[AXIS]
    return jax.shard_map(
        functools.partial(body, size),
        mesh=mesh,
        in_specs=in_specs,
        out_specs=out_specs,
        check_vma=False,
    )
```

```python
import functools
import math

import jax
import jax.numpy as jnp
from jax import lax
from jax.experimental import pallas as pl
from jax.experimental.pallas import tpu as pltpu
from jax.sharding import PartitionSpec as P

AXIS = "row"
VMEM = pltpu.VMEM
NT = (((1,), (1,)), ((), ()))


def swap(x, bits, size):
    return lax.ppermute(x, AXIS, [(i, i ^ bits) for i in range(size)])


def exchange(x, step, count, size):
    return [x] + [swap(x, k * step, size) for k in range(1, count)]


def density_kernel(exc_ref, val_ref, cond_ref, out_ref):
    batch, valence, _ = exc_ref.shape
    cond, val = cond_ref[...], val_ref[...].astype(jnp.float32)
    group = math.gcd(batch, 4)
    sums = []
    for first in range(0, batch, group):
        exc = exc_ref[first : first + group].reshape(group * valence, -1)
        mixed = lax.dot_general(exc, cond, NT, preferred_element_type=jnp.float32)
        mixed = mixed.reshape(group, valence, -1) * val[None]
        sums.append(jnp.sum(mixed, axis=1))
    out_ref[...] = jnp.concatenate(sums, axis=0).astype(out_ref.dtype)


def partial_density(exc_t, val_t, cond_all):
    batch, valence, cond_local = exc_t.shape
    points = cond_all.shape[0]
    width = math.gcd(points, 1024)
    return pl.pallas_call(
        density_kernel,
        grid=(points // width,),
        in_specs=[
            pl.BlockSpec(memory_space=VMEM),
            pl.BlockSpec((valence, width), lambda i: (0, i)),
            pl.BlockSpec((width, cond_local), lambda i: (i, 0)),
        ],
        out_specs=pl.BlockSpec((batch, width), lambda i: (0, i)),
        out_shape=jax.ShapeDtypeStruct((batch, points), jnp.bfloat16),
        compiler_params=pltpu.CompilerParams(vmem_limit_bytes=16 << 20),
        cost_estimate=pl.CostEstimate(
            flops=2 * exc_t.size * points,
            bytes_accessed=2 * (exc_t.size + cond_all.size + val_t.size),
            transcendentals=0,
        ),
    )(exc_t, val_t, cond_all)


def action_kernel(z_ref, cond_ref, val_ref, *refs, layers, span):
    fields, (out_ref, held_ref, total_ref, sems) = refs[:layers], refs[layers:]
    batch = held_ref.shape[1]
    valence = val_ref.shape[0]
    for k, field in enumerate(fields):
        held_ref[z_ref[0] ^ k] = field[...].astype(jnp.float32)
    copies = []
    for first in range(0, batch, span):
        sides = []
        for b in range(first, first + span):
            row = jnp.concatenate([held_ref[k, b : b + 1, :] for k in range(layers)], axis=1)
            sides.append((val_ref[...].astype(jnp.float32) * row).astype(jnp.bfloat16))
        weights = jnp.concatenate(sides, axis=0)
        total = lax.dot_general(cond_ref[...], weights, NT, preferred_element_type=jnp.float32)
        for part in range(span):
            total_ref[first + part] = total[:, part * valence : (part + 1) * valence].astype(total_ref.dtype)
        piece = pl.ds(first, span)
        copies.append(pltpu.make_async_copy(total_ref.at[piece], out_ref.at[piece], sems.at[first // span]))
        copies[-1].start()
    for copy in copies:
        copy.wait()


def action_of(z, cond_t, val_t, fields):
    cond_local, points = cond_t.shape
    valence = val_t.shape[0]
    layers, (batch, chunk) = len(fields), fields[0].shape
    span = batch
    while span > 1 and span * valence * points * 2 > 1 << 20:
        span //= 2
    span = math.gcd(batch, span)
    whole = pl.BlockSpec(memory_space=VMEM)
    shape = (batch, cond_local, valence)
    return pl.pallas_call(
        functools.partial(action_kernel, layers=layers, span=span),
        in_specs=[pl.BlockSpec(memory_space=pltpu.SMEM)] + [whole] * (2 + layers),
        out_specs=pl.BlockSpec(memory_space=pl.ANY),
        out_shape=jax.ShapeDtypeStruct(shape, jnp.bfloat16),
        scratch_shapes=[
            pltpu.VMEM((layers, batch, chunk), jnp.float32),
            pltpu.VMEM(shape, jnp.bfloat16),
            pltpu.SemaphoreType.DMA((batch // span,)),
        ],
        compiler_params=pltpu.CompilerParams(vmem_limit_bytes=16 << 20),
        cost_estimate=pl.CostEstimate(
            flops=2 * batch * valence * cond_local * points,
            bytes_accessed=2 * (cond_t.size + val_t.size + batch * cond_local * valence),
            transcendentals=0,
        ),
    )(z, cond_t, val_t, *fields)


def body_whole(size, excitations, valence_orb, conduction_orb, screened):
    batch, cond_local, valence = excitations.shape
    rows = valence_orb.shape[0]
    points = rows * size
    q_size = 1 << ((size.bit_length() - 1) // 2)
    z_size = size // q_size
    index = lax.axis_index(AXIS)
    z, q = index // q_size, index % q_size

    blocks = conduction_orb.reshape(rows, size, cond_local).transpose(1, 0, 2)
    blocks, valence_orb, screened = lax.optimization_barrier((blocks, valence_orb, screened))
    cond_all = lax.all_to_all(blocks, AXIS, split_axis=0, concat_axis=0, tiled=True)
    cond_all = cond_all.reshape(points, cond_local)

    val = jnp.concatenate(exchange(valence_orb, q_size, z_size, size), axis=0)
    val = jnp.stack(exchange(val, 1, q_size, size)).reshape(size, rows, valence)
    val = jnp.concatenate(
        [val[((i % q_size) ^ q) * z_size + ((i // q_size) ^ z)] for i in range(size)], axis=0
    )
    val_t = val.T
    scr = jnp.stack(exchange(screened, 1, q_size, size))
    scr = jnp.concatenate([scr[k ^ q] for k in range(q_size)], axis=0)
    exc_t = excitations.transpose(0, 2, 1)

    density = partial_density(exc_t, val_t, cond_all)
    density = sum(d.astype(jnp.float32) for d in exchange(density, q_size, z_size, size))
    partial = lax.dot_general(
        density.astype(jnp.bfloat16), scr, NT, preferred_element_type=jnp.float32
    )
    sent = partial.astype(jnp.bfloat16)
    field = partial + sum(f.astype(jnp.float32) for f in exchange(sent, 1, q_size, size)[1:])
    fields = exchange(field.astype(jnp.bfloat16), q_size, z_size, size)
    return action_of(z.reshape(1), cond_all.T, val_t, fields)


def pack_kernel(index_ref, *refs, width):
    *slabs, near_ref, far_ref = refs
    half = len(slabs) // 2
    other = pl.ds(pl.multiple_of((1 - index_ref[0] % 2) * width, 128), width)
    valence = near_ref.shape[1] // half - width
    for k in range(half):
        near_ref[:, k * width : (k + 1) * width] = slabs[k][:, other]
        far_ref[:, k * width : (k + 1) * width] = slabs[half + k][:, other]
        at = half * width + k * valence
        near_ref[:, at : at + valence] = slabs[k][:, 2 * width : 2 * width + valence]
    at = half * width
    for slab in slabs[:half]:
        columns = slab.shape[1] - 2 * width - valence
        if columns:
            far_ref[:, at : at + columns] = slab[:, 2 * width + valence :]
            at += columns


def pack(index, slabs, width, valence):
    half, rows = len(slabs) // 2, slabs[0].shape[0]
    whole = pl.BlockSpec(memory_space=VMEM)
    extra = sum(slab.shape[1] - 2 * (width + valence) for slab in slabs[:half])
    columns = (half * (width + 2 * valence), half * width + extra)
    return pl.pallas_call(
        functools.partial(pack_kernel, width=width),
        in_specs=[pl.BlockSpec(memory_space=pltpu.SMEM)] + [whole] * len(slabs),
        out_specs=[whole] * 2,
        out_shape=[jax.ShapeDtypeStruct((rows, n), slabs[0].dtype) for n in columns],
        compiler_params=pltpu.CompilerParams(vmem_limit_bytes=8 << 20),
        cost_estimate=pl.CostEstimate(flops=0, bytes_accessed=1 << 20, transcendentals=0),
    )(index, *slabs)


def density_part_kernel(index_ref, *refs, straight):
    exc_ref, sources, (out_ref, cond_ref, val_ref) = refs[0], refs[1:-3], refs[-3:]
    batch, valence, width = exc_ref.shape
    rows = sources[0].shape[0]
    blocks = cond_ref.shape[0] // rows
    mine = pl.ds(pl.multiple_of(index_ref[0] % 2 * width, 128), width)
    val = []
    for k in range(blocks):
        if straight:
            half = blocks // 2
            cond = sources[k][:, mine]
            val_source, start = sources[k % half], 2 * width + k // half * valence
        else:
            cond = sources[-1][:, k * width : (k + 1) * width]
            val_source, start = sources[0], blocks * width + (2 * k + len(sources) - 1) * valence
        cond_ref[k * rows : (k + 1) * rows, :] = cond
        val.append(val_source[:, start : start + valence])
    val = jnp.concatenate(val, axis=0).T
    val_ref[...] = val
    val = val.astype(jnp.float32)
    part = math.gcd(batch, 4)
    sums = []
    for first in range(0, batch, part):
        exc = exc_ref[first : first + part].reshape(part * valence, width)
        mixed = lax.dot_general(exc, cond_ref[...], NT, preferred_element_type=jnp.float32)
        mixed = mixed.reshape(part, valence, -1) * val[None]
        sums.append(jnp.sum(mixed, axis=1))
    out_ref[...] = jnp.concatenate(sums, axis=0).astype(out_ref.dtype)


def density_part(index, exc_t, sources, blocks, straight):
    batch, valence, width = exc_t.shape
    points = blocks * sources[0].shape[0]
    whole = pl.BlockSpec(memory_space=VMEM)
    shapes = [(batch, points), (points, width), (valence, points)]
    return pl.pallas_call(
        functools.partial(density_part_kernel, straight=straight),
        in_specs=[pl.BlockSpec(memory_space=pltpu.SMEM)] + [whole] * (1 + len(sources)),
        out_specs=[whole] * len(shapes),
        out_shape=[jax.ShapeDtypeStruct(shape, jnp.bfloat16) for shape in shapes],
        compiler_params=pltpu.CompilerParams(vmem_limit_bytes=16 << 20),
        cost_estimate=pl.CostEstimate(
            flops=2 * exc_t.size * points, bytes_accessed=2 * exc_t.size, transcendentals=0
        ),
    )(index, exc_t, *sources)


def turned(x, flag):
    return jnp.where(flag, jnp.concatenate([x[:, x.shape[1] // 2 :], x[:, : x.shape[1] // 2]], axis=1), x)


def field_kernel(index_ref, *refs, z_size, near, start, rows):
    densities, screened, (forwarded, out_ref, held_ref) = refs[:z_size], refs[z_size:-3], refs[-3:]
    points = held_ref.shape[1]
    pair, chips = 2 * rows, points // (2 * rows)
    chip, core = index_ref[0] // 2, index_ref[0] % 2
    for k in range(chips):
        total = None
        for layer in range(z_size):
            at = (k ^ (layer * near)) * rows
            ref = densities[layer]
            halves = [ref[:, at + c * points // 2 : at + c * points // 2 + rows] for c in range(2)]
            term = jnp.concatenate(halves, axis=1).astype(jnp.float32)
            total = term if total is None else total + term
        place = pl.ds(pl.multiple_of((chip ^ k) * pair, pair), pair)
        held_ref[:, place] = turned(total, core == 1)
    total = held_ref[...]
    high = total.astype(jnp.bfloat16)
    low = (total - high.astype(jnp.float32)).astype(jnp.bfloat16)
    density = jnp.concatenate([high, low], axis=0)
    batch = high.shape[0]
    for k in range(near):
        slab = screened[k]
        at = start + k * points
        both = [slab[:, slab.shape[1] - points :], forwarded[:, at : at + points]]
        both = jnp.concatenate(both, axis=0)
        partial = lax.dot_general(density, both, NT, preferred_element_type=jnp.float32)
        partial = partial[:batch] + partial[batch:]
        place = pl.ds(pl.multiple_of(((chip % near) ^ k) * pair, pair), pair)
        out_ref[:, place] = turned(partial, core == 1).astype(out_ref.dtype)


def field_of(index, densities, screened, forwarded, start):
    batch, points = densities[0].shape
    near, rows = len(screened), screened[0].shape[0]
    whole = pl.BlockSpec(memory_space=VMEM)
    columns = 2 * near * rows
    return pl.pallas_call(
        functools.partial(field_kernel, z_size=len(densities), near=near, start=start, rows=rows),
        in_specs=[pl.BlockSpec(memory_space=pltpu.SMEM)] + [whole] * (len(densities) + near + 1),
        out_specs=whole,
        out_shape=jax.ShapeDtypeStruct((batch, columns), jnp.bfloat16),
        scratch_shapes=[pltpu.VMEM((batch, points), jnp.float32)],
        compiler_params=pltpu.CompilerParams(vmem_limit_bytes=16 << 20),
        cost_estimate=pl.CostEstimate(
            flops=2 * batch * points * columns, bytes_accessed=2 * points * columns, transcendentals=0
        ),
    )(index, *densities, *screened, forwarded)


def project_kernel(index_ref, *refs, layers, parts, span):
    fields, refs = refs[:layers], refs[layers:]
    conds, vals = refs[:parts], refs[parts : 2 * parts]
    out_ref, pairs_ref, total_ref, sems = refs[2 * parts :]
    batch, chunk = fields[0].shape
    chips, _, pair = pairs_ref.shape
    near, valence = chunk // pair, vals[0].shape[0]
    chip, core = index_ref[0] // 2, index_ref[0] % 2
    for layer, ref in enumerate(fields):
        for k in range(near):
            pairs_ref[(chip // near ^ layer) * near + k] = ref[:, k * pair : (k + 1) * pair].astype(jnp.float32)
    both = [turned(pairs_ref[chip ^ k], core == 1) for k in range(chips)]
    halves = [x[:, : pair // 2] for x in both] + [x[:, pair // 2 :] for x in both]
    field = jnp.concatenate(halves, axis=1)
    field = field.astype(jnp.bfloat16).astype(jnp.float32)
    copies = []
    for first in range(0, batch, span):
        total, at = None, 0
        for cond, val in zip(conds, vals):
            stop = at + val.shape[1]
            sides = [
                (val[...].astype(jnp.float32) * field[b : b + 1, at:stop]).astype(jnp.bfloat16)
                for b in range(first, first + span)
            ]
            weights = jnp.concatenate(sides, axis=0)
            term = jnp.dot(weights, cond[...], preferred_element_type=jnp.float32)
            total, at = term if total is None else total + term, stop
        total = total.astype(total_ref.dtype)
        for part in range(span):
            b = first + part
            total_ref[b] = total[part * valence : (part + 1) * valence].T
            copies.append(pltpu.make_async_copy(total_ref.at[b], out_ref.at[b], sems.at[b]))
            copies[-1].start()
    for copy in copies:
        copy.wait()


def project(index, fields, conds, vals, size):
    batch = fields[0].shape[0]
    points, width = sum(cond.shape[0] for cond in conds), conds[0].shape[1]
    valence, span = vals[0].shape[0], math.gcd(batch, 4)
    whole = pl.BlockSpec(memory_space=VMEM)
    shape = (batch, width, valence)
    return pl.pallas_call(
        functools.partial(project_kernel, layers=len(fields), parts=len(conds), span=span),
        in_specs=[pl.BlockSpec(memory_space=pltpu.SMEM)] + [whole] * (len(fields) + 2 * len(conds)),
        out_specs=pl.BlockSpec(memory_space=pl.ANY),
        out_shape=jax.ShapeDtypeStruct(shape, jnp.bfloat16),
        scratch_shapes=[
            pltpu.VMEM((size // 2, batch, 2 * points // size), jnp.float32),
            pltpu.VMEM(shape, jnp.bfloat16),
            pltpu.SemaphoreType.DMA((batch,)),
        ],
        compiler_params=pltpu.CompilerParams(vmem_limit_bytes=16 << 20),
        cost_estimate=pl.CostEstimate(
            flops=2 * batch * valence * width * points,
            bytes_accessed=2 * batch * width * valence,
            transcendentals=0,
        ),
    )(index, *fields, *conds, *vals)


def body_slabs(size, excitations, valence_orb, conduction_orb, screened):
    batch, width, valence = excitations.shape
    q_size = 1 << ((size.bit_length() - 1) // 2)
    z_size = size // q_size
    chips = size // 2
    index = lax.axis_index(AXIS)
    place = index.reshape(1)

    half, near = chips // 2, q_size // 2
    exc_t = excitations.transpose(0, 2, 1)

    def columns(x, k):
        return lax.dynamic_slice_in_dim(x, (index // 2 ^ k) * 2 * width, 2 * width, 1)

    lead = columns(conduction_orb, chips - 1)
    lead, conduction_orb, valence_orb = lax.optimization_barrier((lead, conduction_orb, valence_orb))
    far = [columns(conduction_orb, k) for k in range(half, chips - 1)] + [lead]
    far = [swap(far[k - half], 2 * k, size) for k in range(half, chips)]
    crossed = swap(valence_orb, 2 * half, size)
    crossed, conduction_orb = lax.optimization_barrier((crossed, conduction_orb))
    close = []
    for k in range(half):
        parts = [columns(conduction_orb, k), valence_orb, crossed] + [screened] * (k < near)
        close.append(jnp.concatenate(parts, axis=1))
    slabs = close[:1] + [swap(close[k], 2 * k, size) for k in range(1, half)] + far

    exc_t, *slabs = lax.optimization_barrier((exc_t, *slabs))
    near_part, far_part = pack(place, slabs, width, valence)
    near_part, far_part = swap(near_part, 1, size), swap(far_part, 1, size)
    parts = [
        density_part(place, exc_t, slabs, chips, True),
        density_part(place, exc_t, [near_part], half, False),
        density_part(place, exc_t, [near_part, far_part], half, False),
    ]
    density, conds, vals = [list(x) for x in zip(*parts)]
    density = jnp.concatenate(density, axis=1)

    densities = exchange(density, q_size, z_size, size)
    partial = field_of(place, densities, slabs[:near], far_part, half * width)
    field = sum(x.astype(jnp.float32) for x in exchange(partial, 1, q_size, size)).astype(jnp.bfloat16)
    return project(place, exchange(field, q_size, z_size, size), conds, vals, size)


def body(size, excitations, valence_orb, conduction_orb, screened):
    powers = size >= 8 and size & (size - 1) == 0
    aligned = excitations.shape[1] % 128 == 0 and (2 * valence_orb.shape[0]) % 128 == 0
    run = body_slabs if powers and aligned else body_whole
    return run(size, excitations, valence_orb, conduction_orb, screened)


def solution(mesh):
    in_specs = (
        P("grp", "row", None),
        P(("grp", "row"), None),
        P(("grp", "row"), None),
        P(("grp", "row"), None),
    )
    out_specs = P("grp", "row", None)
    size = mesh.shape[AXIS]
    return jax.shard_map(
        functools.partial(body, size),
        mesh=mesh,
        in_specs=in_specs,
        out_specs=out_specs,
        check_vma=False,
    )
```

```python
import functools
import math

import jax
import jax.numpy as jnp
from jax import lax
from jax.experimental import pallas as pl
from jax.experimental.pallas import tpu as pltpu
from jax.sharding import PartitionSpec as P

AXIS = "row"
VMEM = pltpu.VMEM
NT = (((1,), (1,)), ((), ()))


def swap(x, bits, size):
    return lax.ppermute(x, AXIS, [(i, i ^ bits) for i in range(size)])


def exchange(x, step, count, size):
    return [x] + [swap(x, k * step, size) for k in range(1, count)]


def density_kernel(exc_ref, val_ref, cond_ref, out_ref):
    batch, valence, _ = exc_ref.shape
    cond, val = cond_ref[...], val_ref[...].astype(jnp.float32)
    group = math.gcd(batch, 4)
    sums = []
    for first in range(0, batch, group):
        exc = exc_ref[first : first + group].reshape(group * valence, -1)
        mixed = lax.dot_general(exc, cond, NT, preferred_element_type=jnp.float32)
        mixed = mixed.reshape(group, valence, -1) * val[None]
        sums.append(jnp.sum(mixed, axis=1))
    out_ref[...] = jnp.concatenate(sums, axis=0).astype(out_ref.dtype)


def partial_density(exc_t, val_t, cond_all):
    batch, valence, cond_local = exc_t.shape
    points = cond_all.shape[0]
    width = math.gcd(points, 1024)
    return pl.pallas_call(
        density_kernel,
        grid=(points // width,),
        in_specs=[
            pl.BlockSpec(memory_space=VMEM),
            pl.BlockSpec((valence, width), lambda i: (0, i)),
            pl.BlockSpec((width, cond_local), lambda i: (i, 0)),
        ],
        out_specs=pl.BlockSpec((batch, width), lambda i: (0, i)),
        out_shape=jax.ShapeDtypeStruct((batch, points), jnp.bfloat16),
        compiler_params=pltpu.CompilerParams(vmem_limit_bytes=16 << 20),
        cost_estimate=pl.CostEstimate(
            flops=2 * exc_t.size * points,
            bytes_accessed=2 * (exc_t.size + cond_all.size + val_t.size),
            transcendentals=0,
        ),
    )(exc_t, val_t, cond_all)


def action_kernel(z_ref, cond_ref, val_ref, *refs, layers, span):
    fields, (out_ref, held_ref, total_ref, sems) = refs[:layers], refs[layers:]
    batch = held_ref.shape[1]
    valence = val_ref.shape[0]
    for k, field in enumerate(fields):
        held_ref[z_ref[0] ^ k] = field[...].astype(jnp.float32)
    copies = []
    for first in range(0, batch, span):
        sides = []
        for b in range(first, first + span):
            row = jnp.concatenate([held_ref[k, b : b + 1, :] for k in range(layers)], axis=1)
            sides.append((val_ref[...].astype(jnp.float32) * row).astype(jnp.bfloat16))
        weights = jnp.concatenate(sides, axis=0)
        total = lax.dot_general(cond_ref[...], weights, NT, preferred_element_type=jnp.float32)
        for part in range(span):
            total_ref[first + part] = total[:, part * valence : (part + 1) * valence].astype(total_ref.dtype)
        piece = pl.ds(first, span)
        copies.append(pltpu.make_async_copy(total_ref.at[piece], out_ref.at[piece], sems.at[first // span]))
        copies[-1].start()
    for copy in copies:
        copy.wait()


def action_of(z, cond_t, val_t, fields):
    cond_local, points = cond_t.shape
    valence = val_t.shape[0]
    layers, (batch, chunk) = len(fields), fields[0].shape
    span = batch
    while span > 1 and span * valence * points * 2 > 1 << 20:
        span //= 2
    span = math.gcd(batch, span)
    whole = pl.BlockSpec(memory_space=VMEM)
    shape = (batch, cond_local, valence)
    return pl.pallas_call(
        functools.partial(action_kernel, layers=layers, span=span),
        in_specs=[pl.BlockSpec(memory_space=pltpu.SMEM)] + [whole] * (2 + layers),
        out_specs=pl.BlockSpec(memory_space=pl.ANY),
        out_shape=jax.ShapeDtypeStruct(shape, jnp.bfloat16),
        scratch_shapes=[
            pltpu.VMEM((layers, batch, chunk), jnp.float32),
            pltpu.VMEM(shape, jnp.bfloat16),
            pltpu.SemaphoreType.DMA((batch // span,)),
        ],
        compiler_params=pltpu.CompilerParams(vmem_limit_bytes=16 << 20),
        cost_estimate=pl.CostEstimate(
            flops=2 * batch * valence * cond_local * points,
            bytes_accessed=2 * (cond_t.size + val_t.size + batch * cond_local * valence),
            transcendentals=0,
        ),
    )(z, cond_t, val_t, *fields)


def body_whole(size, excitations, valence_orb, conduction_orb, screened):
    batch, cond_local, valence = excitations.shape
    rows = valence_orb.shape[0]
    points = rows * size
    q_size = 1 << ((size.bit_length() - 1) // 2)
    z_size = size // q_size
    index = lax.axis_index(AXIS)
    z, q = index // q_size, index % q_size

    blocks = conduction_orb.reshape(rows, size, cond_local).transpose(1, 0, 2)
    blocks, valence_orb, screened = lax.optimization_barrier((blocks, valence_orb, screened))
    cond_all = lax.all_to_all(blocks, AXIS, split_axis=0, concat_axis=0, tiled=True)
    cond_all = cond_all.reshape(points, cond_local)

    val = jnp.concatenate(exchange(valence_orb, q_size, z_size, size), axis=0)
    val = jnp.stack(exchange(val, 1, q_size, size)).reshape(size, rows, valence)
    val = jnp.concatenate(
        [val[((i % q_size) ^ q) * z_size + ((i // q_size) ^ z)] for i in range(size)], axis=0
    )
    val_t = val.T
    scr = jnp.stack(exchange(screened, 1, q_size, size))
    scr = jnp.concatenate([scr[k ^ q] for k in range(q_size)], axis=0)
    exc_t = excitations.transpose(0, 2, 1)

    density = partial_density(exc_t, val_t, cond_all)
    density = sum(d.astype(jnp.float32) for d in exchange(density, q_size, z_size, size))
    partial = lax.dot_general(
        density.astype(jnp.bfloat16), scr, NT, preferred_element_type=jnp.float32
    )
    sent = partial.astype(jnp.bfloat16)
    field = partial + sum(f.astype(jnp.float32) for f in exchange(sent, 1, q_size, size)[1:])
    fields = exchange(field.astype(jnp.bfloat16), q_size, z_size, size)
    return action_of(z.reshape(1), cond_all.T, val_t, fields)


def pack_kernel(index_ref, *refs, width):
    *slabs, near_ref, far_ref = refs
    half = len(slabs) // 2
    other = pl.ds(pl.multiple_of((1 - index_ref[0] % 2) * width, 128), width)
    valence = near_ref.shape[1] // half - width
    for k in range(half):
        near_ref[:, k * width : (k + 1) * width] = slabs[k][:, other]
        far_ref[:, k * width : (k + 1) * width] = slabs[half + k][:, other]
        at = half * width + k * valence
        near_ref[:, at : at + valence] = slabs[k][:, 2 * width : 2 * width + valence]
    at = half * width
    for slab in slabs[:half]:
        columns = slab.shape[1] - 2 * width - valence
        if columns:
            far_ref[:, at : at + columns] = slab[:, 2 * width + valence :]
            at += columns


def pack(index, slabs, width, valence):
    half, rows = len(slabs) // 2, slabs[0].shape[0]
    whole = pl.BlockSpec(memory_space=VMEM)
    extra = sum(slab.shape[1] - 2 * (width + valence) for slab in slabs[:half])
    columns = (half * (width + 2 * valence), half * width + extra)
    return pl.pallas_call(
        functools.partial(pack_kernel, width=width),
        in_specs=[pl.BlockSpec(memory_space=pltpu.SMEM)] + [whole] * len(slabs),
        out_specs=[whole] * 2,
        out_shape=[jax.ShapeDtypeStruct((rows, n), slabs[0].dtype) for n in columns],
        compiler_params=pltpu.CompilerParams(vmem_limit_bytes=8 << 20),
        cost_estimate=pl.CostEstimate(flops=0, bytes_accessed=1 << 20, transcendentals=0),
    )(index, *slabs)


def density_part_kernel(index_ref, *refs, straight):
    exc_ref, sources, (out_ref, cond_ref, val_ref) = refs[0], refs[1:-3], refs[-3:]
    batch, valence, width = exc_ref.shape
    rows = sources[0].shape[0]
    blocks = cond_ref.shape[0] // rows
    mine = pl.ds(pl.multiple_of(index_ref[0] % 2 * width, 128), width)
    val = []
    for k in range(blocks):
        if straight:
            half = blocks // 2
            cond = sources[k][:, mine]
            val_source, start = sources[k % half], 2 * width + k // half * valence
        else:
            cond = sources[-1][:, k * width : (k + 1) * width]
            val_source, start = sources[0], blocks * width + (2 * k + len(sources) - 1) * valence
        cond_ref[k * rows : (k + 1) * rows, :] = cond
        val.append(val_source[:, start : start + valence])
    val = jnp.concatenate(val, axis=0).T
    val_ref[...] = val
    val = val.astype(jnp.float32)
    part = math.gcd(batch, 4)
    sums = []
    for first in range(0, batch, part):
        exc = exc_ref[first : first + part].reshape(part * valence, width)
        mixed = lax.dot_general(exc, cond_ref[...], NT, preferred_element_type=jnp.float32)
        mixed = mixed.reshape(part, valence, -1) * val[None]
        sums.append(jnp.sum(mixed, axis=1))
    out_ref[...] = jnp.concatenate(sums, axis=0).astype(out_ref.dtype)


def density_part(index, exc_t, sources, blocks, straight):
    batch, valence, width = exc_t.shape
    points = blocks * sources[0].shape[0]
    whole = pl.BlockSpec(memory_space=VMEM)
    shapes = [(batch, points), (points, width), (valence, points)]
    return pl.pallas_call(
        functools.partial(density_part_kernel, straight=straight),
        in_specs=[pl.BlockSpec(memory_space=pltpu.SMEM)] + [whole] * (1 + len(sources)),
        out_specs=[whole] * len(shapes),
        out_shape=[jax.ShapeDtypeStruct(shape, jnp.bfloat16) for shape in shapes],
        compiler_params=pltpu.CompilerParams(vmem_limit_bytes=16 << 20),
        cost_estimate=pl.CostEstimate(
            flops=2 * exc_t.size * points, bytes_accessed=2 * exc_t.size, transcendentals=0
        ),
    )(index, exc_t, *sources)


def turned(x, flag):
    return jnp.where(flag, jnp.concatenate([x[:, x.shape[1] // 2 :], x[:, : x.shape[1] // 2]], axis=1), x)


def field_kernel(index_ref, *refs, z_size, near, start, rows):
    densities, screened, (forwarded, out_ref, held_ref) = refs[:z_size], refs[z_size:-3], refs[-3:]
    points = held_ref.shape[1]
    pair, chips = 2 * rows, points // (2 * rows)
    chip, core = index_ref[0] // 2, index_ref[0] % 2
    for k in range(chips):
        total = None
        for layer in range(z_size):
            at = (k ^ (layer * near)) * rows
            ref = densities[layer]
            halves = [ref[:, at + c * points // 2 : at + c * points // 2 + rows] for c in range(2)]
            term = jnp.concatenate(halves, axis=1).astype(jnp.float32)
            total = term if total is None else total + term
        place = pl.ds(pl.multiple_of((chip ^ k) * pair, pair), pair)
        held_ref[:, place] = turned(total, core == 1)
    total = held_ref[...]
    high = total.astype(jnp.bfloat16)
    low = (total - high.astype(jnp.float32)).astype(jnp.bfloat16)
    density = jnp.concatenate([high, low], axis=0)
    batch = high.shape[0]
    for k in range(near):
        slab = screened[k]
        at = start + k * points
        both = [slab[:, slab.shape[1] - points :], forwarded[:, at : at + points]]
        both = jnp.concatenate(both, axis=0)
        partial = lax.dot_general(density, both, NT, preferred_element_type=jnp.float32)
        partial = partial[:batch] + partial[batch:]
        place = pl.ds(pl.multiple_of(((chip % near) ^ k) * pair, pair), pair)
        out_ref[:, place] = turned(partial, core == 1).astype(out_ref.dtype)


def field_of(index, densities, screened, forwarded, start):
    batch, points = densities[0].shape
    near, rows = len(screened), screened[0].shape[0]
    whole = pl.BlockSpec(memory_space=VMEM)
    columns = 2 * near * rows
    return pl.pallas_call(
        functools.partial(field_kernel, z_size=len(densities), near=near, start=start, rows=rows),
        in_specs=[pl.BlockSpec(memory_space=pltpu.SMEM)] + [whole] * (len(densities) + near + 1),
        out_specs=whole,
        out_shape=jax.ShapeDtypeStruct((batch, columns), jnp.bfloat16),
        scratch_shapes=[pltpu.VMEM((batch, points), jnp.float32)],
        compiler_params=pltpu.CompilerParams(vmem_limit_bytes=16 << 20),
        cost_estimate=pl.CostEstimate(
            flops=2 * batch * points * columns, bytes_accessed=2 * points * columns, transcendentals=0
        ),
    )(index, *densities, *screened, forwarded)


def project_kernel(index_ref, *refs, layers, parts, span):
    fields, refs = refs[:layers], refs[layers:]
    conds, vals = refs[:parts], refs[parts : 2 * parts]
    out_ref, pairs_ref, total_ref, sems = refs[2 * parts :]
    batch, chunk = fields[0].shape
    chips, _, pair = pairs_ref.shape
    near, valence = chunk // pair, vals[0].shape[0]
    chip, core = index_ref[0] // 2, index_ref[0] % 2
    for layer, ref in enumerate(fields):
        for k in range(near):
            pairs_ref[(chip // near ^ layer) * near + k] = ref[:, k * pair : (k + 1) * pair].astype(jnp.float32)
    both = [turned(pairs_ref[chip ^ k], core == 1) for k in range(chips)]
    halves = [x[:, : pair // 2] for x in both] + [x[:, pair // 2 :] for x in both]
    field = jnp.concatenate(halves, axis=1)
    field = field.astype(jnp.bfloat16).astype(jnp.float32)
    copies = []
    for first in range(0, batch, span):
        total, at = None, 0
        for cond, val in zip(conds, vals):
            stop = at + val.shape[1]
            sides = [
                (val[...].astype(jnp.float32) * field[b : b + 1, at:stop]).astype(jnp.bfloat16)
                for b in range(first, first + span)
            ]
            weights = jnp.concatenate(sides, axis=0)
            term = jnp.dot(weights, cond[...], preferred_element_type=jnp.float32)
            total, at = term if total is None else total + term, stop
        total = total.astype(total_ref.dtype)
        for part in range(span):
            b = first + part
            total_ref[b] = total[part * valence : (part + 1) * valence].T
            copies.append(pltpu.make_async_copy(total_ref.at[b], out_ref.at[b], sems.at[b]))
            copies[-1].start()
    for copy in copies:
        copy.wait()


def project(index, fields, conds, vals, size):
    batch = fields[0].shape[0]
    points, width = sum(cond.shape[0] for cond in conds), conds[0].shape[1]
    valence, span = vals[0].shape[0], math.gcd(batch, 4)
    whole = pl.BlockSpec(memory_space=VMEM)
    shape = (batch, width, valence)
    return pl.pallas_call(
        functools.partial(project_kernel, layers=len(fields), parts=len(conds), span=span),
        in_specs=[pl.BlockSpec(memory_space=pltpu.SMEM)] + [whole] * (len(fields) + 2 * len(conds)),
        out_specs=pl.BlockSpec(memory_space=pl.ANY),
        out_shape=jax.ShapeDtypeStruct(shape, jnp.bfloat16),
        scratch_shapes=[
            pltpu.VMEM((size // 2, batch, 2 * points // size), jnp.float32),
            pltpu.VMEM(shape, jnp.bfloat16),
            pltpu.SemaphoreType.DMA((batch,)),
        ],
        compiler_params=pltpu.CompilerParams(vmem_limit_bytes=16 << 20),
        cost_estimate=pl.CostEstimate(
            flops=2 * batch * valence * width * points,
            bytes_accessed=2 * batch * width * valence,
            transcendentals=0,
        ),
    )(index, *fields, *conds, *vals)


def body_slabs(size, excitations, valence_orb, conduction_orb, screened):
    batch, width, valence = excitations.shape
    q_size = 1 << ((size.bit_length() - 1) // 2)
    z_size = size // q_size
    chips = size // 2
    index = lax.axis_index(AXIS)
    place = index.reshape(1)

    half, near = chips // 2, q_size // 2
    exc_t = excitations.transpose(0, 2, 1)

    def columns(x, k):
        return lax.dynamic_slice_in_dim(x, (index // 2 ^ k) * 2 * width, 2 * width, 1)

    lead = columns(conduction_orb, chips - 1)
    far = [columns(conduction_orb, k) for k in range(half, chips - 1)] + [lead]
    far = [swap(far[k - half], 2 * k, size) for k in range(half, chips)]
    crossed = swap(valence_orb, 2 * half, size)
    crossed, conduction_orb = lax.optimization_barrier((crossed, conduction_orb))
    close = []
    for k in range(half):
        parts = [columns(conduction_orb, k), valence_orb, crossed] + [screened] * (k < near)
        close.append(jnp.concatenate(parts, axis=1))
    slabs = close[:1] + [swap(close[k], 2 * k, size) for k in range(1, half)] + far

    exc_t, *slabs = lax.optimization_barrier((exc_t, *slabs))
    near_part, far_part = pack(place, slabs, width, valence)
    near_part, far_part = swap(near_part, 1, size), swap(far_part, 1, size)
    parts = [
        density_part(place, exc_t, slabs, chips, True),
        density_part(place, exc_t, [near_part], half, False),
        density_part(place, exc_t, [near_part, far_part], half, False),
    ]
    density, conds, vals = [list(x) for x in zip(*parts)]
    density = jnp.concatenate(density, axis=1)

    densities = exchange(density, q_size, z_size, size)
    partial = field_of(place, densities, slabs[:near], far_part, half * width)
    field = sum(x.astype(jnp.float32) for x in exchange(partial, 1, q_size, size)).astype(jnp.bfloat16)
    return project(place, exchange(field, q_size, z_size, size), conds, vals, size)


def body(size, excitations, valence_orb, conduction_orb, screened):
    powers = size >= 8 and size & (size - 1) == 0
    aligned = excitations.shape[1] % 128 == 0 and (2 * valence_orb.shape[0]) % 128 == 0
    run = body_slabs if powers and aligned else body_whole
    return run(size, excitations, valence_orb, conduction_orb, screened)


def solution(mesh):
    in_specs = (
        P("grp", "row", None),
        P(("grp", "row"), None),
        P(("grp", "row"), None),
        P(("grp", "row"), None),
    )
    out_specs = P("grp", "row", None)
    size = mesh.shape[AXIS]
    return jax.shard_map(
        functools.partial(body, size),
        mesh=mesh,
        in_specs=in_specs,
        out_specs=out_specs,
        check_vma=False,
    )
```
